512 devices in a mesh: dp: 8 (over x, core), tensor: 64 (over z, y).
Axes of the slice: x: 4, y: 8, z: 8, core: 2. Of those that a mesh axis runs over, the one named last changes fastest.
Arguments:
- embeddings: bfloat16 [65536, 3584], P('tensor', 'dp'), may hold values from -8 to 8
- pairs: int32 [3072, 2], replicated, may hold values from 0 to 511, as said below
- partner: int32 [65536], P('tensor'), may hold values from 0 to 65535, as said below
Outputs:
- lse_terms: float32 [65536], P('tensor')
- embedding_grad: bfloat16 [65536, 3584], P('tensor', 'dp')
The draws below stay inside these ranges and needn't reach their ends.
Inputs may be any that keep to these rules, and one draw needn't show every extreme that they name: `pairs`: rows 48 * g to 48 * g + 47 belong to tensor index g, which holds blocks g * 8 to g * 8 + 7. In each of these rows the first block is one of index g's blocks and the second block is held by another tensor index; no two rows of one index name second blocks held by the same index. partner[i] lies in i's block, differs from i, and partner[partner[i]] = i.
All inputs are finite; a program needn't handle non-finite values.
Results may differ from the reference program's by a relative error of at most 0.0036.
Values may be sent and summed in bfloat16 or wider, within the bound.
A program may use at most 128 MiB of HBM per device.

```python
import math
import jax
import jax.numpy as jnp
from jax import lax

D = 3584
BLK = 128
BPD = 8
NBLK = 512
TEXTS = 65536
NPAIR = 3072
N_TENSOR = 64


def draw_embeddings(key, part):
    key = jax.random.fold_in(key, 23)
    values = jax.random.truncated_normal(key, -6.0, 6.0, (TEXTS, D), jnp.float32)
    return values.astype(jnp.bfloat16)


def draw_pairs(key, part):
    key = jax.random.fold_in(key, 11)
    per_group = NPAIR // N_TENSOR

    def one_group(group_idx):
        group_key = jax.random.fold_in(key, group_idx)
        key_perm, key_col, key_row = jax.random.split(group_key, 3)
        offsets = jax.random.permutation(key_perm, N_TENSOR - 1)[:per_group] + 1
        owners = (group_idx + offsets) % N_TENSOR
        second = owners * BPD + jax.random.randint(key_col, (per_group,), 0, BPD)
        first = group_idx * BPD + jax.random.randint(key_row, (per_group,), 0, BPD)
        return jnp.stack([first, second], axis=1)
    table = jax.vmap(one_group)(jnp.arange(N_TENSOR, dtype=jnp.int32))
    return table.reshape(NPAIR, 2).astype(jnp.int32)


def draw_partner(key, part):
    key = jax.random.fold_in(key, 37)

    def one_block(block_idx):
        order = jax.random.permutation(jax.random.fold_in(key, block_idx), BLK)
        evens = order[0::2]
        odds = order[1::2]
        local = jnp.zeros((BLK,), jnp.int32).at[evens].set(odds).at[odds].set(evens)
        return local + block_idx * BLK
    table = jax.vmap(one_block)(jnp.arange(NBLK, dtype=jnp.int32))
    return table.reshape(TEXTS).astype(jnp.int32)


def setup_inputs(seed: int = 0) -> dict:
    seeds = jax.random.split(jax.random.key(seed), 4)
    embeddings = draw_embeddings(jax.random.fold_in(seeds[3], 71), 0)
    pairs = draw_pairs(jax.random.fold_in(seeds[3], 71), 0)
    partner = draw_partner(jax.random.fold_in(seeds[3], 71), 0)
    return {"embeddings": embeddings, "pairs": pairs, "partner": partner}


NEG = -1e+30

def row_lse(values, axis):
    top = lax.optimization_barrier(jnp.max(values, axis=axis, keepdims=True))
    total = lax.optimization_barrier(jnp.sum(jnp.exp(values - top), axis=axis, keepdims=True))
    return jnp.squeeze(top + jnp.log(total), axis=axis)

def reference(embeddings, pairs, partner):
    logit_scale = 2.0 / math.sqrt(D)
    nblocks = TEXTS // BLK
    blocks = embeddings.reshape(nblocks, BLK, D)
    self_mask = jnp.eye(BLK, dtype=bool)

    def tile_scores(left, right):
        return logit_scale * jnp.dot(left, right.T, preferred_element_type=jnp.float32)

    def diag_scores(block):
        return jnp.where(self_mask, jnp.float32(NEG), tile_scores(block, block))
    diag_lse = lax.map(lambda block: row_lse(diag_scores(block), 1), blocks)

    def pair_stats(pair):
        first = jnp.take(blocks, pair[0], axis=0)
        second = jnp.take(blocks, pair[1], axis=0)
        scores = tile_scores(first, second)
        return (row_lse(scores, 1), row_lse(scores, 0))
    row_part, col_part = lax.map(pair_stats, pairs)
    values = jnp.concatenate([diag_lse, row_part, col_part], axis=0)
    owners = jnp.concatenate([jnp.arange(nblocks, dtype=jnp.int32), pairs[:, 0], pairs[:, 1]]).astype(jnp.int32)
    top = jnp.full((nblocks, BLK), NEG, jnp.float32).at[owners].max(values)
    total = jnp.zeros((nblocks, BLK), jnp.float32).at[owners].add(jnp.exp(values - top[owners]))
    lse_blocks = top + jnp.log(total)

    def diag_grad(index):
        block = jnp.take(blocks, index, axis=0)
        level = jnp.take(lse_blocks, index, axis=0)
        scores = diag_scores(block)
        weights = (jnp.exp(scores - level[:, None]) + jnp.exp(scores - level[None, :])).astype(jnp.bfloat16)
        return jnp.dot(weights, block, preferred_element_type=jnp.float32)
    grads = lax.map(diag_grad, jnp.arange(nblocks, dtype=jnp.int32))

    def pair_grad(running, pair):
        first = jnp.take(blocks, pair[0], axis=0)
        second = jnp.take(blocks, pair[1], axis=0)
        level_first = jnp.take(lse_blocks, pair[0], axis=0)
        level_second = jnp.take(lse_blocks, pair[1], axis=0)
        scores = tile_scores(first, second)
        weights = (jnp.exp(scores - level_first[:, None]) + jnp.exp(scores - level_second[None, :])).astype(jnp.bfloat16)
        running = running.at[pair[0]].add(jnp.dot(weights, second, preferred_element_type=jnp.float32))
        running = running.at[pair[1]].add(jnp.dot(weights.T, first, preferred_element_type=jnp.float32))
        return (running, None)
    grads, _ = lax.scan(pair_grad, grads, pairs)
    partner_rows = jnp.take(embeddings, partner, axis=0).astype(jnp.float32)
    embedding_grad = (grads.reshape(TEXTS, D) - 2.0 * partner_rows).astype(jnp.bfloat16)
    return (lse_blocks.reshape(TEXTS), embedding_grad)
```

```python
import math

import jax
import jax.numpy as jnp
from jax import lax
from jax.sharding import PartitionSpec as P

D = 3584
BPD = 8
NEG = -1e30


def merged_lse(values, axis):
    top = jnp.max(values, axis=axis, keepdims=True)
    total = jnp.sum(jnp.exp(values - top), axis=axis, keepdims=True)
    return jnp.squeeze(top + jnp.log(total), axis=axis)


def slot_tables(pairs, group_idx, side):
    groups = side * side
    per_group = pairs.shape[0] // groups
    z_here, y_here = group_idx // side, group_idx % side
    rows = lax.dynamic_slice_in_dim(
        pairs.reshape(side, side, per_group, 2), z_here, 1, 0
    )[0]
    owner = rows[:, :, 1] // BPD
    wanted = jnp.arange(side) * side + y_here
    match = owner[:, None, :] == wanted[None, :, None]
    first = jnp.sum(jnp.where(match, rows[:, None, :, 0] % BPD, 0), axis=2)
    second = jnp.sum(jnp.where(match, rows[:, None, :, 1] % BPD, 0), axis=2)
    return first, second, jnp.any(match, axis=2)


def per_device(embeddings, pairs, partner):
    rows_here, width_dev = embeddings.shape
    groups = lax.axis_size("tensor")
    side = math.isqrt(groups)
    group_idx = lax.axis_index("tensor")
    block_len = rows_here // BPD
    logit_scale = 2.0 / math.sqrt(D)
    along_y = [[z * side + y for y in range(side)] for z in range(side)]
    along_z = [[z * side + y for z in range(side)] for y in range(side)]
    own_blocks = embeddings.reshape(BPD, block_len, width_dev)
    first, second, valid = slot_tables(pairs, group_idx, side)

    row_blocks = lax.all_gather(own_blocks, "tensor", axis_index_groups=along_y)
    col_blocks = lax.all_gather(own_blocks, "tensor", axis_index_groups=along_z)
    diag_partial = jnp.einsum(
        "kiw,kjw->kij", own_blocks, own_blocks, preferred_element_type=jnp.float32
    )
    lane = jnp.arange(side)
    first_rows = row_blocks[lane[:, None], first]
    second_rows = col_blocks[lane[None, :], second]
    pair_partial = jnp.einsum(
        "yziw,yzjw->yzij", first_rows, second_rows, preferred_element_type=jnp.float32
    )
    diag_summed, pair_summed = lax.psum((diag_partial, pair_partial), "dp")
    self_mask = jnp.eye(block_len, dtype=bool)[None, :, :]
    diag_scores = jnp.where(self_mask, jnp.float32(NEG), logit_scale * diag_summed)
    pair_scores = logit_scale * pair_summed
    diag_lse = merged_lse(diag_scores, 2)
    row_part = merged_lse(pair_scores, 3)
    col_part = merged_lse(pair_scores, 2)
    ids = jnp.arange(BPD)
    row_hot = (first[:, :, None] == ids) & valid[:, :, None]
    col_hot = (second[:, :, None] == ids) & valid[:, :, None]
    row_stats = merged_lse(
        jnp.where(row_hot[..., None], row_part[:, :, None, :], jnp.float32(NEG)), 1
    )
    col_stats = merged_lse(
        jnp.where(col_hot[..., None], col_part[:, :, None, :], jnp.float32(NEG)), 0
    )
    row_in = lax.all_to_all(
        row_stats, "tensor", 0, 0, axis_index_groups=along_y, tiled=True
    )
    col_in = lax.all_to_all(
        col_stats, "tensor", 0, 0, axis_index_groups=along_z, tiled=True
    )
    lse_own = merged_lse(jnp.concatenate([diag_lse[None], row_in, col_in], axis=0), 0)
    row_lse = lax.all_gather(lse_own, "tensor", axis_index_groups=along_y)
    col_lse = lax.all_gather(lse_own, "tensor", axis_index_groups=along_z)
    row_level = row_lse[lane[:, None], first]
    col_level = col_lse[lane[None, :], second]
    diag_weights = (
        jnp.exp(diag_scores - lse_own[:, :, None]) + jnp.exp(diag_scores - lse_own[:, None, :])
    ).astype(jnp.bfloat16)
    pair_weights = jnp.where(
        valid[:, :, None, None],
        jnp.exp(pair_scores - row_level[..., :, None])
        + jnp.exp(pair_scores - col_level[..., None, :]),
        0.0,
    ).astype(jnp.bfloat16)
    diag_terms = jnp.einsum(
        "kij,kjw->kiw", diag_weights, own_blocks, preferred_element_type=jnp.float32
    )
    zero = jnp.bfloat16(0)
    wide_row = jnp.where(row_hot[..., None, None], pair_weights[:, :, None], zero)
    wide_col = jnp.where(col_hot[..., None, None], pair_weights[:, :, None], zero)
    row_terms = jnp.einsum(
        "yzkij,yzjw->ykiw", wide_row, second_rows, preferred_element_type=jnp.float32
    ).astype(jnp.bfloat16)
    col_terms = jnp.einsum(
        "yzkij,yziw->zkjw", wide_col, first_rows, preferred_element_type=jnp.float32
    ).astype(jnp.bfloat16)
    row_grad = lax.psum_scatter(row_terms, "tensor", axis_index_groups=along_y)
    col_grad = lax.psum_scatter(col_terms, "tensor", axis_index_groups=along_z)
    total = diag_terms + row_grad.astype(jnp.float32) + col_grad.astype(jnp.float32)
    total = total.reshape(rows_here, width_dev)
    partner_local = partner - group_idx * rows_here
    partner_rows = jnp.take(embeddings, partner_local, axis=0).astype(jnp.float32)
    embedding_grad = (total - 2.0 * partner_rows).astype(jnp.bfloat16)
    return (lse_own.reshape(rows_here), embedding_grad)


def solution(mesh):
    in_specs = (P("tensor", "dp"), P(), P("tensor"))
    out_specs = (P("tensor"), P("tensor", "dp"))
    return jax.shard_map(
        per_device, mesh=mesh, in_specs=in_specs, out_specs=out_specs, check_vma=False
    )
```

```python
import functools
import math

import jax
import jax.numpy as jnp
from jax import lax
from jax.experimental import pallas as pl
from jax.experimental.pallas import tpu as pltpu
from jax.sharding import PartitionSpec as P

D = 3584
BPD = 8
BLK = 128
HALF_BPD = BPD // 2
NEG = -1e30
VMEM_BYTES = 63 * 1024 * 1024
MESH = pl.DeviceIdType.MESH
F32 = jnp.float32
BF16 = jnp.bfloat16


def ring_distance(rel, side):
    return min(rel, side - rel)


def slot_plan(side):
    batches = []
    for step in range(1, side // 2 + 1):
        batches.append(
            [
                (ry, rz)
                for ry in range(side)
                for rz in range(side)
                if max(ring_distance(ry, side), ring_distance(rz, side)) == step
            ]
        )
    return batches


def slot_tables(pairs, group_idx, side):
    groups = side * side
    per_group = pairs.shape[0] // groups
    z_here, y_here = group_idx // side, group_idx % side
    rows = lax.dynamic_slice_in_dim(
        pairs.reshape(side, side, per_group, 2), z_here, 1, 0
    )[0]
    order = [slot for batch in slot_plan(side) for slot in batch]
    ry = jnp.array([slot[0] for slot in order], jnp.int32)
    rz = jnp.array([slot[1] for slot in order], jnp.int32)
    source = rows[(y_here + ry) % side]
    wanted = ((z_here + rz) % side) * side + y_here
    match = source[:, :, 1] // BPD == wanted[:, None]
    listed = jnp.any(match, axis=1)
    first = jnp.sum(jnp.where(match, source[:, :, 0] % BPD, 0), axis=1)
    second = jnp.sum(jnp.where(match, source[:, :, 1] % BPD, 0), axis=1)
    first = jnp.where(listed, first, -1)
    second = jnp.where(listed, second, -1)
    return jnp.stack([first, second, ry, rz]).astype(jnp.int32)


def lse_rows(values):
    top = jnp.max(values, axis=0, keepdims=True)
    return top + jnp.log(jnp.sum(jnp.exp(values - top), axis=0, keepdims=True))


def merge(parts):
    top = functools.reduce(jnp.maximum, parts)
    return top + jnp.log(functools.reduce(jnp.add, [jnp.exp(p - top) for p in parts]))


def kernel(side, xs, scale, *refs):
    half = side // 2
    plan = slot_plan(side)
    counts = [BPD] + [len(batch) for batch in plan]
    nb = len(counts)
    pos = {slot: i for i, slot in enumerate(s for batch in plan for s in batch)}
    base = [0]
    for batch in plan:
        base.append(base[-1] + len(batch))
    events = 2 * half - 1

    refs = list(refs)

    def take(n):
        out = refs[:n]
        del refs[:n]
        return out

    emb, tab, partner, lse_out, grad_out = take(5)
    rowbuf = [emb] + take(side - 1)
    colbuf = [emb] + take(side - 1)
    part = take(nb)
    from_core = take(nb)
    from_x = take(nb)
    score = take(nb)
    (row_stat, col_stat, diag_stat, stat_send, stat_recv, level, w_ref, wt_ref) = take(8)
    (wide, stacked, temp, acc, fresh) = take(5)
    ring_in = [take(events) for _ in range(4)]
    (ag_send, ag_recv, c1_send, c1_recv, x2_send, x2_recv, x3_send, x3_recv) = take(8)
    (c4_send, c4_recv, l_send, l_recv, rs_send, rs_recv) = take(6)

    me = lax.axis_index("tensor")
    d = lax.axis_index("dp")
    z_here, y_here = lax.div(me, side), lax.rem(me, side)
    x_here, core = lax.div(d, 2), lax.rem(d, 2)
    other = 1 - core

    def at_y(r):
        return {"dp": d, "tensor": z_here * side + lax.rem(y_here + r, side)}

    def at_z(r):
        return {"dp": d, "tensor": lax.rem(z_here + r, side) * side + y_here}

    def x_of(r):
        return lax.rem(x_here + r, xs)

    def at_x(r):
        return {"dp": x_of(r) * 2 + core, "tensor": me}

    at_core = {"dp": x_here * 2 + other, "tensor": me}
    peers = [at_y(r) for r in range(1, side)] + [at_z(r) for r in range(1, side)]
    peers += [at_x(r) for r in range(1, xs)] + [at_core]
    barrier = pltpu.get_barrier_semaphore()
    for peer in peers:
        pl.semaphore_signal(barrier, inc=1, device_id=peer, device_id_type=MESH)
    pl.semaphore_wait(barrier, len(peers))

    started = []

    def send(src, dst, send_sem, recv_sem, device):
        copy = pltpu.make_async_remote_copy(
            src_ref=src,
            dst_ref=dst,
            send_sem=send_sem,
            recv_sem=recv_sem,
            device_id=device,
            device_id_type=MESH,
        )
        copy.start()
        started.append(copy)
        return copy

    flows = [(0, 1), (0, -1), (1, 1), (1, -1)]
    bufs = [rowbuf, colbuf]
    ahead = [at_y, at_z]

    def chunk_of(sign, e):
        first = 0 if sign > 0 else 1
        return first if e % 2 == 0 else 1 - first

    def chunk(ref, c):
        return ref.at[pl.ds(c * HALF_BPD, HALF_BPD)]

    gathers = [[None] * events for _ in flows]

    def gather_send(e):
        for f, (axis, sign) in enumerate(flows):
            s, c = e // 2, chunk_of(sign, e)
            gathers[f][e] = send(
                chunk(bufs[axis][(-s * sign) % side], c),
                chunk(bufs[axis][(-(s + 1) * sign) % side], c),
                ag_send.at[f, e],
                ag_recv.at[f, e],
                ahead[axis](sign % side),
            )

    inflight = {}
    rows_x = BLK // (2 * xs)

    def dot_nt(a, b):
        return lax.dot_general(a, b, (((1,), (1,)), ((), ())), preferred_element_type=F32)

    def partial_scores(b):
        if b == 0:
            for k in range(BPD):
                s = dot_nt(emb[k], emb[k])
                part[b][:, :, k] = s.reshape(2, xs, rows_x, BLK)
            return
        for t, (ry, rz) in enumerate(plan[b - 1]):
            p = base[b - 1] + t
            first = jnp.maximum(tab[0, p], 0)
            second = jnp.maximum(tab[1, p], 0)
            s = dot_nt(rowbuf[ry][first], colbuf[rz][second])
            part[b][:, :, t] = s.reshape(2, xs, rows_x, BLK)

    def stage1(b):
        inflight[b] = [
            send(part[b].at[other], from_core[b], c1_send.at[b], c1_recv.at[b], at_core)
        ]

    def stage2(b):
        inflight[b][0].wait_recv()
        part[b][core] = part[b][core] + from_core[b][...]
        inflight[b] = [
            send(
                part[b].at[core, x_of(r)],
                from_x[b].at[r - 1],
                x2_send.at[b, r - 1],
                x2_recv.at[b, r - 1],
                at_x(r),
            )
            for r in range(1, xs)
        ]

    def stage3(b):
        for copy in inflight[b]:
            copy.wait_recv()
        total = part[b][core, x_here]
        for r in range(1, xs):
            total = total + from_x[b][r - 1]
        score[b][core, x_here] = total * scale
        mine = score[b].at[core, x_here]
        inflight[b] = [
            send(mine, mine, x3_send.at[b, r - 1], x3_recv.at[b, r - 1], at_x(r))
            for r in range(1, xs)
        ]

    def stage4(b):
        for copy in inflight[b]:
            copy.wait_recv()
        inflight[b] = [
            send(score[b].at[core], score[b].at[core], c4_send.at[b], c4_recv.at[b], at_core)
        ]

    def tile(b, t):
        return score[b][:, :, t].reshape(BLK, BLK)

    eye = lax.broadcasted_iota(jnp.int32, (BLK, BLK), 0) == lax.broadcasted_iota(
        jnp.int32, (BLK, BLK), 1
    )

    def stage5(b):
        inflight[b][0].wait_recv()
        if b == 0:

            def diag_body(t, carry):
                values = jnp.where(eye, NEG, tile(0, t))
                diag_stat[pl.ds(t, 1), :] = lse_rows(values)
                return carry

            lax.fori_loop(0, counts[0], diag_body, 0)
            return

        def body(t, carry):
            values = tile(b, t)
            col_stat[pl.ds(base[b - 1] + t, 1), :] = lse_rows(values)
            row_stat[pl.ds(base[b - 1] + t, 1), :] = lse_rows(values.T)
            return carry

        lax.fori_loop(0, counts[b], body, 0)

    stages = [stage1, stage2, stage3, stage4, stage5]
    progress = {}

    def tick():
        for b in sorted(progress):
            if progress[b] < len(stages):
                stages[progress[b]](b)
                progress[b] += 1

    gather_send(0)
    if events > 1:
        gather_send(1)
    partial_scores(0)
    progress[0] = 0
    tick()
    for e in range(events):
        for f in range(4):
            gathers[f][e].wait_recv()
        if e + 2 < events:
            gather_send(e + 2)
        b = half if e == events - 1 else ((e + 1) // 2 if e % 2 == 1 else 0)
        if b:
            partial_scores(b)
            progress[b] = 0
        tick()
    while any(p < len(stages) for p in progress.values()):
        tick()

    block_id = lax.broadcasted_iota(jnp.int32, (BPD, BLK), 0)
    for axis, stat in ((0, row_stat), (1, col_stat)):
        for r in range(side):
            found = []
            for o in range(side):
                if (r, o) == (0, 0):
                    continue
                p = pos[(r, o) if axis == 0 else (o, r)]
                line = jnp.broadcast_to(stat[pl.ds(p, 1), :], (BPD, BLK))
                found.append(jnp.where(block_id == tab[axis, p], line, NEG))
            stat_send[axis, r] = merge(found)
    exchanged = []
    for axis in (0, 1):
        for r in range(1, side):
            exchanged.append(
                send(
                    stat_send.at[axis, r],
                    stat_recv.at[axis, (-r) % side],
                    l_send.at[0, axis, r],
                    l_recv.at[0, axis, r],
                    ahead[axis](r),
                )
            )
    for copy in exchanged:
        copy.wait_recv()
    found = [diag_stat[...], stat_send[0, 0], stat_send[1, 0]]
    for axis in (0, 1):
        found += [stat_recv[axis, r] for r in range(1, side)]
    lse_own = merge(found)
    lse_out[...] = lse_own
    level[0, 0] = lse_own
    level[1, 0] = lse_own
    exchanged = []
    for axis in (0, 1):
        for r in range(1, side):
            exchanged.append(
                send(
                    level.at[axis, 0],
                    level.at[axis, (-r) % side],
                    l_send.at[1, axis, r],
                    l_recv.at[1, axis, r],
                    ahead[axis](r),
                )
            )
    for copy in exchanged:
        copy.wait_recv()

    def two_sided(values, li, lj):
        li = jnp.broadcast_to(li, (BLK, BLK)).T
        return jnp.exp(values - li) + jnp.exp(values - lj)

    def weights(b):
        def body(t, carry):
            p = base[b - 1] + t
            first, second = tab[0, p], tab[1, p]
            li = level[0, tab[2, p], pl.ds(jnp.maximum(first, 0), 1), :]
            lj = level[1, tab[3, p], pl.ds(jnp.maximum(second, 0), 1), :]
            w = jnp.where(first >= 0, two_sided(tile(b, t), li, lj), 0.0)
            w_ref[p] = w.astype(BF16)
            wt_ref[p] = w.T.astype(BF16)
            return carry

        lax.fori_loop(0, counts[b], body, 0)

    def contribution(axis, rel, c):
        slots = [o for o in range(side) if (rel, o) != (0, 0)]
        for i, o in enumerate(slots):
            p = pos[(rel, o) if axis == 0 else (o, rel)]
            mine, theirs = tab[axis, p], tab[1 - axis, p]
            lanes = pl.ds(i * BLK, BLK)
            stacked[lanes, :] = bufs[1 - axis][o][jnp.maximum(theirs, 0)]
            w = (w_ref if axis == 0 else wt_ref)[p]
            for k in range(HALF_BPD):
                wide[pl.ds(k * BLK, BLK), lanes] = jnp.where(
                    mine == c * HALF_BPD + k, w, jnp.zeros_like(w)
                )
        depth = pl.ds(0, len(slots) * BLK)
        return jnp.dot(wide[:, depth], stacked[depth, :], preferred_element_type=F32)

    shape = (HALF_BPD, BLK, emb.shape[2])
    scatters = [[None] * events for _ in flows]
    for e in range(events):
        rho = half - (e + 1) // 2
        if e == 0 or e % 2 == 1:
            weights(rho)
        for f, (axis, sign) in enumerate(flows):
            temp[f] = contribution(axis, (rho * sign) % side, chunk_of(sign, e)).reshape(shape)
        for f, (axis, sign) in enumerate(flows):
            if e < 2:
                out = fresh.at[f, e]
                out[...] = temp[f].astype(BF16)
            else:
                scatters[f][e - 2].wait_recv()
                out = ring_in[f][e - 2]
                out[...] = (temp[f] + out[...].astype(F32)).astype(BF16)
            scatters[f][e] = send(
                out, ring_in[f][e], rs_send.at[f, e], rs_recv.at[f, e], ahead[axis](sign % side)
            )

    for k in range(BPD):
        line = lse_own[k : k + 1]
        values = jnp.where(eye, NEG, tile(0, k))
        w = two_sided(values, line, line).astype(BF16)
        swap = lax.broadcasted_iota(jnp.int32, (BLK, BLK), 0) == partner[pl.ds(k, 1), :]
        swap = jnp.where(swap, 1.0, 0.0).astype(BF16)
        acc[k] = jnp.dot(w, emb[k], preferred_element_type=F32) - 2.0 * jnp.dot(
            swap, emb[k], preferred_element_type=F32
        )
    for axis in (0, 1):
        for c in (0, 1):
            rows = pl.ds(c * HALF_BPD, HALF_BPD)
            acc[rows] = acc[rows] + contribution(axis, 0, c).reshape(shape)
    last = [e for e in range(events) if half - (e + 1) // 2 == 1]
    for e in last:
        for f, (axis, sign) in enumerate(flows):
            scatters[f][e].wait_recv()
            rows = pl.ds(chunk_of(sign, e) * HALF_BPD, HALF_BPD)
            acc[rows] = acc[rows] + ring_in[f][e][...].astype(F32)
    grad_out[...] = acc[...].astype(BF16)
    for copy in started:
        copy.wait_send()


def fused(embeddings, tab, partner, side, xs):
    _, _, width = embeddings.shape
    half = side // 2
    plan = slot_plan(side)
    counts = [BPD] + [len(batch) for batch in plan]
    nb = len(counts)
    nslot = sum(counts[1:])
    events = 2 * half - 1
    rows_x = BLK // (2 * xs)
    dma = pltpu.SemaphoreType.DMA
    blocks = pltpu.VMEM((BPD, BLK, width), BF16)
    chunk = pltpu.VMEM((HALF_BPD, BLK, width), BF16)
    stats = pltpu.VMEM((2, side, BPD, BLK), F32)
    scratch = [blocks] * (2 * (side - 1))
    scratch += [pltpu.VMEM((2, xs, n, rows_x, BLK), F32) for n in counts]
    scratch += [pltpu.VMEM((xs, n, rows_x, BLK), F32) for n in counts]
    scratch += [pltpu.VMEM((max(xs - 1, 1), n, rows_x, BLK), F32) for n in counts]
    scratch += [pltpu.VMEM((2, xs, n, rows_x, BLK), F32) for n in counts]
    padded = -(-nslot // 8) * 8
    scratch += [pltpu.VMEM((padded, BLK), F32)] * 2 + [pltpu.VMEM((BPD, BLK), F32)]
    scratch += [stats] * 3 + [pltpu.VMEM((nslot, BLK, BLK), BF16)] * 2
    scratch += [
        pltpu.VMEM((HALF_BPD * BLK, side * BLK), BF16),
        pltpu.VMEM((side * BLK, width), BF16),
        pltpu.VMEM((4, HALF_BPD, BLK, width), F32),
        pltpu.VMEM((BPD, BLK, width), F32),
        pltpu.VMEM((4, 2, HALF_BPD, BLK, width), BF16),
    ]
    scratch += [chunk] * (4 * events)
    scratch += [dma((4, events))] * 2 + [dma((nb,))] * 2 + [dma((nb, max(xs - 1, 1)))] * 4
    scratch += [dma((nb,))] * 2 + [dma((2, 2, side))] * 2 + [dma((4, events))] * 2
    vmem = pl.BlockSpec(memory_space=pltpu.VMEM)
    flops = 2 * BLK * BLK * width * (counts[0] * 4 + nslot * (1 + 2 * BPD))
    return pl.pallas_call(
        functools.partial(kernel, side, xs, 2.0 / math.sqrt(D)),
        out_shape=(
            jax.ShapeDtypeStruct((BPD, BLK), F32),
            jax.ShapeDtypeStruct((BPD, BLK, width), BF16),
        ),
        in_specs=[vmem, pl.BlockSpec(memory_space=pltpu.SMEM), vmem],
        out_specs=(vmem, vmem),
        scratch_shapes=scratch,
        compiler_params=pltpu.CompilerParams(
            collective_id=0, has_side_effects=True, vmem_limit_bytes=VMEM_BYTES
        ),
        cost_estimate=pl.CostEstimate(
            flops=flops, bytes_accessed=4 * embeddings.size, transcendentals=6 * nslot * BLK * BLK
        ),
    )(embeddings, tab, partner)


def per_device(embeddings, pairs, partner):
    rows_here, width = embeddings.shape
    side = math.isqrt(lax.axis_size("tensor"))
    xs = lax.axis_size("dp") // 2
    tab = slot_tables(pairs, lax.axis_index("tensor"), side)
    lse, grad = fused(
        embeddings.reshape(BPD, BLK, width),
        tab,
        (partner % BLK).reshape(BPD, BLK),
        side,
        xs,
    )
    return lse.reshape(rows_here), grad.reshape(rows_here, width)


def solution(mesh):
    in_specs = (P("tensor", "dp"), P(), P("tensor"))
    out_specs = (P("tensor"), P("tensor", "dp"))
    return jax.shard_map(
        per_device, mesh=mesh, in_specs=in_specs, out_specs=out_specs, check_vma=False
    )
```

```python
import functools
import math

import jax
import jax.numpy as jnp
import numpy as np
from jax import lax
from jax.experimental import pallas as pl
from jax.experimental.pallas import tpu as pltpu
from jax.sharding import PartitionSpec as P

D = 3584
BPD = 8
BLK = 128
HALF_BPD = BPD // 2
NEG = -1e30
VMEM_BYTES = 63 * 1024 * 1024
MESH = pl.DeviceIdType.MESH
F32 = jnp.float32
BF16 = jnp.bfloat16


def ring_distance(rel, side):
    return min(rel, side - rel)


def slot_plan(side):
    batches = []
    for step in range(1, side // 2 + 1):
        batches.append(
            [
                (ry, rz)
                for ry in range(side)
                for rz in range(side)
                if max(ring_distance(ry, side), ring_distance(rz, side)) == step
            ]
        )
    return batches


def slot_grid(side):
    order = [slot for batch in slot_plan(side) for slot in batch]
    grid = np.zeros((-(-len(order) // 8) * 8, BLK), np.int32)
    grid[: len(order), :2] = order
    return grid


def lse_rows(values):
    top = jnp.max(values, axis=0, keepdims=True)
    return top + jnp.log(jnp.sum(jnp.exp(values - top), axis=0, keepdims=True))


def merge(parts):
    top = functools.reduce(jnp.maximum, parts)
    return top + jnp.log(functools.reduce(jnp.add, [jnp.exp(p - top) for p in parts]))


def kernel(side, xs, scale, *refs):
    half = side // 2
    plan = slot_plan(side)
    counts = [BPD] + [len(batch) for batch in plan]
    nb = len(counts)
    pos = {slot: i for i, slot in enumerate(s for batch in plan for s in batch)}
    base = [0]
    for batch in plan:
        base.append(base[-1] + len(batch))
    events = 2 * half - 1

    refs = list(refs)

    def take(n):
        out = refs[:n]
        del refs[:n]
        return out

    emb, pairs, partner, grid, lse_out, grad_out = take(6)
    (own,) = take(1)
    rowbuf = [own] + take(side - 1)
    colbuf = [own] + take(side - 1)
    part = take(nb)
    from_core = take(nb)
    from_x = take(nb)
    score = take(nb)
    (row_stat, col_stat, diag_stat, stat_send, stat_recv, level, w_ref, wt_ref) = take(8)
    (keys, dp_stat) = take(2)
    (wide, stacked, temp, acc, fresh, done, tab_vmem, tab) = take(8)
    ring_in = [take(events) for _ in range(4)]
    (ag_send, ag_recv, c1_send, c1_recv) = take(4)
    x_sems = take(2)
    (c4_send, c4_recv, l_send, l_recv, rs_send, rs_recv, in_sem, out_sem, tab_sem) = take(9)
    dp_sems = take(2)

    me = lax.axis_index("tensor")
    d = lax.axis_index("dp")
    z_here, y_here = lax.div(me, side), lax.rem(me, side)
    x_here, core = lax.div(d, 2), lax.rem(d, 2)
    other = 1 - core

    def at_y(r):
        return {"dp": d, "tensor": z_here * side + lax.rem(y_here + r, side)}

    def at_z(r):
        return {"dp": d, "tensor": lax.rem(z_here + r, side) * side + y_here}

    def x_of(r):
        return lax.rem(x_here + r + xs, xs)

    def at_x(r):
        return {"dp": x_of(r) * 2 + core, "tensor": me}

    def at_dp(r):
        return {"dp": lax.rem(d + r, 2 * xs), "tensor": me}

    at_core = {"dp": x_here * 2 + other, "tensor": me}
    peers = [at_y(r) for r in range(1, side)] + [at_z(r) for r in range(1, side)]
    peers += [at_dp(r) for r in range(1, 2 * xs)]
    loads = [
        pltpu.make_async_copy(emb.at[:, pl.ds(k * BLK, BLK)], own.at[k], in_sem.at[k])
        for k in range(BPD)
    ]
    for copy in loads:
        copy.start()
    barrier = pltpu.get_barrier_semaphore()
    for peer in peers:
        pl.semaphore_signal(barrier, inc=1, device_id=peer, device_id_type=MESH)
    for copy in loads:
        copy.wait()
    pl.semaphore_wait(barrier, len(peers))

    started = []

    def send(src, dst, send_sem, recv_sem, device):
        copy = pltpu.make_async_remote_copy(
            src_ref=src,
            dst_ref=dst,
            send_sem=send_sem,
            recv_sem=recv_sem,
            device_id=device,
            device_id_type=MESH,
        )
        copy.start()
        started.append(copy)
        return copy

    flows = [(0, 1), (0, -1), (1, 1), (1, -1)]
    bufs = [rowbuf, colbuf]
    ahead = [at_y, at_z]

    def chunk_of(sign, e):
        first = 0 if sign > 0 else 1
        return first if e % 2 == 0 else 1 - first

    def chunk(ref, c):
        return ref.at[pl.ds(c * HALF_BPD, HALF_BPD)]

    gathers = [[None] * events for _ in flows]

    def gather_send(e):
        for f, (axis, sign) in enumerate(flows):
            s, c = e // 2, chunk_of(sign, e)
            gathers[f][e] = send(
                chunk(bufs[axis][(-s * sign) % side], c),
                chunk(bufs[axis][(-(s + 1) * sign) % side], c),
                ag_send.at[f, e],
                ag_recv.at[f, e],
                ahead[axis](sign % side),
            )

    inflight = {}
    rows_x = BLK // (2 * xs)
    per_line = BLK // rows_x
    group0 = [0, 0]
    for n in counts[1:]:
        group0.append(group0[-1] + -(-n // per_line))

    def dot_tn(a, b):
        return lax.dot_general(a, b, (((0,), (0,)), ((), ())), preferred_element_type=F32)

    def slot_tables():
        ry, rz = grid[:, 0:1], grid[:, 1:2]
        source = z_here * side + lax.rem(y_here + ry, side)
        wanted = lax.rem(z_here + rz, side) * side + y_here
        npair = pairs.shape[1]
        per_group = npair // (side * side)
        lane = lax.broadcasted_iota(jnp.int32, (grid.shape[0], npair), 1)
        low = source * per_group
        match = (lane >= low) & (lane < low + per_group)
        match = match & (lax.shift_right_logical(pairs[1:2, :], 3) == wanted)
        first = jnp.max(jnp.where(match, pairs[0:1, :] & 7, -1), axis=1, keepdims=True)
        second = jnp.max(jnp.where(match, pairs[1:2, :] & 7, -1), axis=1, keepdims=True)
        column = lax.broadcasted_iota(jnp.int32, (grid.shape[0], BLK), 1)
        tab_vmem[...] = jnp.where(
            column == 0, first, jnp.where(column == 1, second, jnp.where(column == 2, ry, rz))
        )
        copy = pltpu.make_async_copy(tab_vmem, tab, tab_sem)
        copy.start()
        copy.wait()
        lane_tile = lax.broadcasted_iota(jnp.int32, (1, BLK), 1) // rows_x
        for b in range(1, nb):
            for t in range(counts[b]):
                p = base[b - 1] + t
                first = tab[p, 0]
                key = jnp.where(first >= 0, first + BPD * tab[p, 2], -1)
                line = pl.ds(group0[b] + t // per_line, 1)
                held = jnp.full((1, BLK), -1, jnp.int32) if t % per_line == 0 else keys[line, :]
                keys[line, :] = jnp.where(lane_tile == t % per_line, key, held)

    def partial_scores(b):
        if b == 0:
            for k in range(BPD):
                s = dot_tn(own[k], own[k])
                part[b][:, :, k] = s.reshape(2, xs, rows_x, BLK)
            return
        for t, (ry, rz) in enumerate(plan[b - 1]):
            p = base[b - 1] + t
            first = jnp.maximum(tab[p, 0], 0)
            second = jnp.maximum(tab[p, 1], 0)
            s = dot_tn(rowbuf[ry][first], colbuf[rz][second])
            part[b][:, :, t] = s.reshape(2, xs, rows_x, BLK)

    def stage1(b):
        inflight[b] = [
            send(part[b].at[other], from_core[b], c1_send.at[b], c1_recv.at[b], at_core)
        ]

    def x_send(b, i, src, dst, r):
        return send(src, dst, x_sems[0].at[b, i], x_sems[1].at[b, i], at_x(r))

    def stage2(b):
        inflight[b][0].wait_recv()
        part[b][core] = part[b][core] + from_core[b][...]
        inflight[b] = [
            x_send(b, r, part[b].at[core, x_of(r)], from_x[b].at[r - 1], r) for r in range(1, xs)
        ]

    def reduce_rows(b):
        for copy in inflight[b]:
            copy.wait_recv()
        total = part[b][core, x_here]
        for r in range(1, xs):
            total = total + from_x[b][r - 1]
        score[b][core, x_here] = total * scale

    def spread_rows(b):
        mine = score[b].at[core, x_here]
        inflight[b] = [x_send(b, xs + r, mine, mine, r) for r in range(1, xs)]

    def row_partials(b):
        mine = score[b][core, x_here]
        n = counts[b]
        if b == 0:
            row = lax.broadcasted_iota(jnp.int32, mine.shape, 1) + (core * xs + x_here) * rows_x
            values = jnp.where(row == lax.broadcasted_iota(jnp.int32, mine.shape, 2), NEG, mine)
        else:
            values = mine
        top = jnp.max(values, axis=1, keepdims=True)
        total = jnp.sum(jnp.exp(values - top), axis=1, keepdims=True)
        cols = (top + jnp.log(total)).reshape(n, BLK)
        if b == 0:
            diag_stat[...] = cols
            return
        col_stat[pl.ds(base[b - 1], n), :] = cols
        flat = mine.reshape(n * rows_x, BLK)
        for g in range(-(-n // per_line)):
            lines = flat[g * BLK : (g + 1) * BLK]
            if lines.shape[0] < BLK:
                lines = jnp.concatenate([lines, jnp.zeros((BLK - lines.shape[0], BLK), F32)], axis=0)
            row_stat[pl.ds(group0[b] + g, 1), :] = lse_rows(lines.T)

    def stage3(b):
        reduce_rows(b)
        spread_rows(b)
        row_partials(b)

    def stage4(b):
        for copy in inflight[b]:
            copy.wait_recv()
        inflight[b] = [
            send(score[b].at[core], score[b].at[core], c4_send.at[b], c4_recv.at[b], at_core)
        ]

    def stage5(b):
        inflight[b][0].wait_recv()

    def tile(b, t):
        return score[b][:, :, t].reshape(BLK, BLK)

    eye = lax.broadcasted_iota(jnp.int32, (BLK, BLK), 0) == lax.broadcasted_iota(
        jnp.int32, (BLK, BLK), 1
    )

    stages = [stage1, stage2, stage3, stage4, stage5]
    progress = {}

    def tick():
        for b in sorted(progress):
            if progress[b] < len(stages):
                stages[progress[b]](b)
                progress[b] += 1

    gather_send(0)
    if events > 1:
        gather_send(1)
    partial_scores(0)
    progress[0] = 0
    tick()
    slot_tables()
    tick()
    for e in range(events):
        for f in range(4):
            gathers[f][e].wait_recv()
        if e + 2 < events:
            gather_send(e + 2)
        b = half if e == events - 1 else ((e + 1) // 2 if e % 2 == 1 else 0)
        if b:
            partial_scores(b)
            if b >= half - 1:
                stage1(b)
                stage2(b)
            else:
                progress[b] = 0
        tick()
        tick()
    while any(p < len(stages) for p in progress.values()):
        tick()
    tail = [b for b in (half - 1, half) if b >= 1]
    for b in tail:
        reduce_rows(b)
        if b == half:
            for late in reversed(tail):
                spread_rows(late)
        row_partials(b)

    block_id = lax.broadcasted_iota(jnp.int32, (BPD, BLK), 0)

    def over_lanes(values, combine):
        shift = BLK // 2
        while shift >= rows_x:
            values = combine(values, pltpu.roll(values, shift, 1))
            shift //= 2
        return values

    def exchange(step, axis, source, slots):
        return [
            send(
                source(r),
                slots.at[axis, (-r) % side],
                l_send.at[step, axis, r],
                l_recv.at[step, axis, r],
                ahead[axis](r),
            )
            for r in range(1, side)
        ]

    for r in range(side):
        found = []
        for o in range(side):
            if (r, o) == (0, 0):
                continue
            p = pos[(o, r)]
            line = jnp.broadcast_to(col_stat[pl.ds(p, 1), :], (BPD, BLK))
            found.append(jnp.where(block_id == tab[p, 1], line, NEG))
        stat_send[1, r] = merge(found)
    exchanged = exchange(0, 1, lambda r: stat_send.at[1, r], stat_recv)
    for r in range(side):
        found = []
        for g in range(group0[-1]):
            line = jnp.broadcast_to(row_stat[pl.ds(g, 1), :], (BPD, BLK))
            key = jnp.broadcast_to(keys[pl.ds(g, 1), :], (BPD, BLK))
            found.append(jnp.where(key == block_id + BPD * r, line, NEG))
        top = over_lanes(functools.reduce(jnp.maximum, found), jnp.maximum)
        total = functools.reduce(jnp.add, [jnp.exp(v - top) for v in found])
        stat_send[0, r] = top + jnp.log(over_lanes(total, jnp.add))
    exchanged += exchange(0, 0, lambda r: stat_send.at[0, r], stat_recv)
    for copy in exchanged:
        copy.wait_recv()
    dp_stat[0, 0] = merge([stat_send[0, 0]] + [stat_recv[0, r] for r in range(1, side)])
    dp_stat[0, 1] = merge(
        [diag_stat[...], stat_send[1, 0]] + [stat_recv[1, r] for r in range(1, side)]
    )
    exchanged = [
        send(
            dp_stat.at[0],
            dp_stat.at[2 * xs - r],
            dp_sems[0].at[r],
            dp_sems[1].at[r],
            at_dp(r),
        )
        for r in range(1, 2 * xs)
    ]
    for copy in exchanged:
        copy.wait_recv()
    lane_group = lax.broadcasted_iota(jnp.int32, (BPD, BLK), 1) // rows_x
    found = []
    for r in range(2 * xs):
        source = lax.rem(d + r, 2 * xs)
        part_of = lax.rem(source, 2) * xs + lax.div(source, 2)
        found.append(jnp.where(lane_group == part_of, dp_stat[r, 0], NEG))
        found.append(dp_stat[r, 1])
    lse_own = merge(found)
    lse_out[...] = lse_own
    level[0, 0] = lse_own
    level[1, 0] = lse_own
    exchanged = exchange(1, 0, lambda r: level.at[0, 0], level)
    exchanged += exchange(1, 1, lambda r: level.at[1, 0], level)
    for stage in (stage4, stage5):
        for b in reversed(tail):
            stage(b)
    for copy in exchanged:
        copy.wait_recv()

    def two_sided(values, li, lj):
        li = jnp.broadcast_to(li, (BLK, BLK)).T
        return jnp.exp(values - li) + jnp.exp(values - lj)

    def weights(b):
        def body(t, carry):
            p = base[b - 1] + t
            first, second = tab[p, 0], tab[p, 1]
            li = level[0, tab[p, 2], pl.ds(jnp.maximum(first, 0), 1), :]
            lj = level[1, tab[p, 3], pl.ds(jnp.maximum(second, 0), 1), :]
            w = jnp.where(first >= 0, two_sided(tile(b, t), li, lj), 0.0)
            w_ref[p] = w.astype(BF16)
            wt_ref[p] = w.T.astype(BF16)
            return carry

        lax.fori_loop(0, counts[b], body, 0)

    def contribution(axis, rel, c):
        slots = [o for o in range(side) if (rel, o) != (0, 0)]
        for i, o in enumerate(slots):
            p = pos[(rel, o) if axis == 0 else (o, rel)]
            mine, theirs = tab[p, axis], tab[p, 1 - axis]
            lanes = pl.ds(i * BLK, BLK)
            stacked[:, lanes] = bufs[1 - axis][o][jnp.maximum(theirs, 0)]
            w = (wt_ref if axis == 0 else w_ref)[p]
            for k in range(HALF_BPD):
                wide[lanes, pl.ds(k * BLK, BLK)] = jnp.where(
                    mine == c * HALF_BPD + k, w, jnp.zeros_like(w)
                )
        depth = pl.ds(0, len(slots) * BLK)
        return jnp.dot(stacked[:, depth], wide[depth, :], preferred_element_type=F32)

    def by_block(out, offset, values):
        for k in range(HALF_BPD):
            out[offset + k] = values[:, k * BLK : (k + 1) * BLK]

    scatters = [[None] * events for _ in flows]
    for e in range(events):
        rho = half - (e + 1) // 2
        if e == 0 or e % 2 == 1:
            weights(rho)
        for f, (axis, sign) in enumerate(flows):
            by_block(temp.at[f], 0, contribution(axis, (rho * sign) % side, chunk_of(sign, e)))
        for f, (axis, sign) in enumerate(flows):
            if e < 2:
                out = fresh.at[f, e]
                out[...] = temp[f].astype(BF16)
            else:
                scatters[f][e - 2].wait_recv()
                out = ring_in[f][e - 2]
                out[...] = (temp[f] + out[...].astype(F32)).astype(BF16)
            scatters[f][e] = send(
                out, ring_in[f][e], rs_send.at[f, e], rs_recv.at[f, e], ahead[axis](sign % side)
            )

    for k in range(BPD):
        line = lse_own[k : k + 1]
        values = jnp.where(eye, NEG, tile(0, k))
        w = two_sided(values, line, line).T.astype(BF16)
        swap = lax.broadcasted_iota(jnp.int32, (BLK, BLK), 0) == partner[pl.ds(k, 1), :]
        swap = jnp.where(swap, 1.0, 0.0).astype(BF16)
        acc[k] = jnp.dot(own[k], w, preferred_element_type=F32) - 2.0 * jnp.dot(
            own[k], swap, preferred_element_type=F32
        )
    for axis in (0, 1):
        for c in (0, 1):
            rows = pl.ds(c * HALF_BPD, HALF_BPD)
            by_block(temp.at[0], 0, contribution(axis, 0, c))
            acc[rows] = acc[rows] + temp[0]
    last = [e for e in range(events) if half - (e + 1) // 2 == 1]
    for e in last:
        for f, (axis, sign) in enumerate(flows):
            scatters[f][e].wait_recv()
            rows = pl.ds(chunk_of(sign, e) * HALF_BPD, HALF_BPD)
            acc[rows] = acc[rows] + ring_in[f][e][...].astype(F32)
    stores = []
    for k in range(BPD):
        done[k] = acc[k].astype(BF16)
        stores.append(
            pltpu.make_async_copy(done.at[k], grad_out.at[:, pl.ds(k * BLK, BLK)], out_sem.at[k])
        )
        stores[k].start()
    for copy in stores:
        copy.wait()
    for copy in started:
        copy.wait_send()


def fused(embeddings, pairs, partner, side, xs):
    width = embeddings.shape[0]
    half = side // 2
    plan = slot_plan(side)
    counts = [BPD] + [len(batch) for batch in plan]
    nb = len(counts)
    nslot = sum(counts[1:])
    events = 2 * half - 1
    rows_x = BLK // (2 * xs)
    dma = pltpu.SemaphoreType.DMA
    blocks = pltpu.VMEM((BPD, width, BLK), BF16)
    chunk = pltpu.VMEM((HALF_BPD, width, BLK), BF16)
    stats = pltpu.VMEM((2, side, BPD, BLK), F32)
    scratch = [blocks] * (2 * side - 1)
    scratch += [pltpu.VMEM((2, xs, n, rows_x, BLK), F32) for n in counts]
    scratch += [pltpu.VMEM((xs, n, rows_x, BLK), F32) for n in counts]
    scratch += [pltpu.VMEM((xs - 1, n, rows_x, BLK), F32) for n in counts]
    scratch += [pltpu.VMEM((2, xs, n, rows_x, BLK), F32) for n in counts]
    padded = -(-nslot // 8) * 8
    scratch += [pltpu.VMEM((padded, BLK), F32)] * 2 + [pltpu.VMEM((BPD, BLK), F32)]
    scratch += [stats] * 3 + [pltpu.VMEM((nslot, BLK, BLK), BF16)] * 2
    scratch += [pltpu.VMEM((padded, BLK), jnp.int32), pltpu.VMEM((2 * xs, 2, BPD, BLK), F32)]
    scratch += [
        pltpu.VMEM((side * BLK, HALF_BPD * BLK), BF16),
        pltpu.VMEM((width, side * BLK), BF16),
        pltpu.VMEM((4, HALF_BPD, width, BLK), F32),
        pltpu.VMEM((BPD, width, BLK), F32),
        pltpu.VMEM((4, 2, HALF_BPD, width, BLK), BF16),
        blocks,
        pltpu.VMEM((padded, BLK), jnp.int32),
        pltpu.SMEM((padded, BLK), jnp.int32),
    ]
    scratch += [chunk] * (4 * events)
    scratch += [dma((4, events))] * 2 + [dma((nb,))] * 2 + [dma((nb, 2 * xs))] * 2
    scratch += [dma((nb,))] * 2 + [dma((2, 2, side))] * 2 + [dma((4, events))] * 2
    scratch += [dma((BPD,))] * 2 + [dma(())] + [dma((2 * xs,))] * 2
    anywhere = pl.BlockSpec(memory_space=pl.ANY)
    vmem = pl.BlockSpec(memory_space=pltpu.VMEM)
    flops = 2 * BLK * BLK * width * (counts[0] * 4 + nslot * (1 + 2 * BPD))
    return pl.pallas_call(
        functools.partial(kernel, side, xs, 2.0 / math.sqrt(D)),
        out_shape=(
            jax.ShapeDtypeStruct((BPD, BLK), F32),
            jax.ShapeDtypeStruct((width, BPD * BLK), BF16),
        ),
        in_specs=[anywhere, vmem, vmem, vmem],
        out_specs=(vmem, anywhere),
        scratch_shapes=scratch,
        compiler_params=pltpu.CompilerParams(
            collective_id=0, has_side_effects=True, vmem_limit_bytes=VMEM_BYTES
        ),
        cost_estimate=pl.CostEstimate(
            flops=flops, bytes_accessed=4 * embeddings.size, transcendentals=6 * nslot * BLK * BLK
        ),
    )(embeddings, pairs, partner, jnp.asarray(slot_grid(side)))


def per_device(embeddings, pairs, partner):
    rows_here, width = embeddings.shape
    side = math.isqrt(lax.axis_size("tensor"))
    xs = lax.axis_size("dp") // 2
    lse, grad = fused(
        embeddings.T, pairs.T, (partner % BLK).reshape(BPD, BLK), side, xs
    )
    return lse.reshape(rows_here), grad.T


def solution(mesh):
    in_specs = (P("tensor", "dp"), P(), P("tensor"))
    out_specs = (P("tensor"), P("tensor", "dp"))
    return jax.shard_map(
        per_device, mesh=mesh, in_specs=in_specs, out_specs=out_specs, check_vma=False
    )
```

```python
import functools
import math

import jax
import jax.numpy as jnp
import numpy as np
from jax import lax
from jax.experimental import pallas as pl
from jax.experimental.pallas import tpu as pltpu
from jax.sharding import PartitionSpec as P

D = 3584
BPD = 8
BLK = 128
HALF_BPD = BPD // 2
NEG = -1e30
VMEM_BYTES = 63 * 1024 * 1024
MESH = pl.DeviceIdType.MESH
F32 = jnp.float32
BF16 = jnp.bfloat16


def ring_distance(rel, side):
    return min(rel, side - rel)


def slot_plan(side):
    batches = []
    for step in range(1, side // 2 + 1):
        batch = [
            (ry, rz)
            for ry in range(side)
            for rz in range(side)
            if max(ring_distance(ry, side), ring_distance(rz, side)) == step
        ]
        batches.append(sorted(batch, key=lambda slot: slot[0] != side // 2))
    return batches


def slot_grid(side):
    order = [slot for batch in slot_plan(side) for slot in batch]
    grid = np.zeros((-(-len(order) // 8) * 8, BLK), np.int32)
    grid[: len(order), :2] = order
    return grid


def lse_rows(values):
    top = jnp.max(values, axis=0, keepdims=True)
    return top + jnp.log(jnp.sum(jnp.exp(values - top), axis=0, keepdims=True))


def merge(parts):
    top = functools.reduce(jnp.maximum, parts)
    return top + jnp.log(functools.reduce(jnp.add, [jnp.exp(p - top) for p in parts]))


def kernel(side, xs, scale, *refs):
    half = side // 2
    plan = slot_plan(side)
    counts = [BPD] + [len(batch) for batch in plan]
    nb = len(counts)
    pos = {slot: i for i, slot in enumerate(s for batch in plan for s in batch)}
    base = [0]
    for batch in plan:
        base.append(base[-1] + len(batch))
    events = 2 * half - 1

    refs = list(refs)

    def take(n):
        out = refs[:n]
        del refs[:n]
        return out

    emb, pairs, partner, grid, lse_out, grad_out = take(6)
    (own,) = take(1)
    rowbuf = [own] + take(side - 1)
    colbuf = [own] + take(side - 1)
    part = take(nb)
    from_core = take(nb)
    from_x = take(nb)
    score = take(nb)
    (row_stat, col_stat, diag_stat, stat_send, stat_recv, level, w_ref, wt_ref) = take(8)
    (keys, dp_stat) = take(2)
    (wide, stacked, temp, acc, fresh, done, tab_vmem, tab) = take(8)
    ring_in = [take(events) for _ in range(4)]
    (ag_send, ag_recv, c1_send, c1_recv) = take(4)
    x_sems = take(2)
    (c4_send, c4_recv, l_send, l_recv, rs_send, rs_recv, in_sem, out_sem, tab_sem) = take(9)
    dp_sems = take(2)

    me = lax.axis_index("tensor")
    d = lax.axis_index("dp")
    z_here, y_here = lax.div(me, side), lax.rem(me, side)
    x_here, core = lax.div(d, 2), lax.rem(d, 2)
    other = 1 - core

    def at_y(r):
        return {"dp": d, "tensor": z_here * side + lax.rem(y_here + r, side)}

    def at_z(r):
        return {"dp": d, "tensor": lax.rem(z_here + r, side) * side + y_here}

    def x_of(r):
        return lax.rem(x_here + r + xs, xs)

    def at_x(r):
        return {"dp": x_of(r) * 2 + core, "tensor": me}

    def at_dp(r):
        return {"dp": lax.rem(d + r, 2 * xs), "tensor": me}

    at_core = {"dp": x_here * 2 + other, "tensor": me}
    peers = [at_y(r) for r in range(1, side)] + [at_z(r) for r in range(1, side)]
    peers += [at_dp(r) for r in range(1, 2 * xs)]
    loads = [
        pltpu.make_async_copy(emb.at[:, pl.ds(k * BLK, BLK)], own.at[k], in_sem.at[k])
        for k in range(BPD)
    ]
    for copy in loads:
        copy.start()
    barrier = pltpu.get_barrier_semaphore()
    for peer in peers:
        pl.semaphore_signal(barrier, inc=1, device_id=peer, device_id_type=MESH)
    for copy in loads:
        copy.wait()
    pl.semaphore_wait(barrier, len(peers))

    started = []

    def send(src, dst, send_sem, recv_sem, device):
        copy = pltpu.make_async_remote_copy(
            src_ref=src,
            dst_ref=dst,
            send_sem=send_sem,
            recv_sem=recv_sem,
            device_id=device,
            device_id_type=MESH,
        )
        copy.start()
        started.append(copy)
        return copy

    flows = [(0, 1), (0, -1), (1, 1), (1, -1)]
    bufs = [rowbuf, colbuf]
    ahead = [at_y, at_z]

    def chunk_of(sign, e):
        first = 0 if sign > 0 else 1
        return first if e % 2 == 0 else 1 - first

    def chunk(ref, c):
        return ref.at[pl.ds(c * HALF_BPD, HALF_BPD)]

    gathers = [[None] * events for _ in flows]

    def gather_send(f, e):
        axis, sign = flows[f]
        s, c = e // 2, chunk_of(sign, e)
        gathers[f][e] = send(
            chunk(bufs[axis][(-s * sign) % side], c),
            chunk(bufs[axis][(-(s + 1) * sign) % side], c),
            ag_send.at[f, e],
            ag_recv.at[f, e],
            ahead[axis](sign % side),
        )

    inflight = {}
    rows_x = BLK // (2 * xs)
    per_line = BLK // rows_x
    group0 = [0, 0]
    for n in counts[1:]:
        group0.append(group0[-1] + -(-n // per_line))

    def dot_tn(a, b):
        return lax.dot_general(a, b, (((0,), (0,)), ((), ())), preferred_element_type=F32)

    def slot_tables():
        ry, rz = grid[:, 0:1], grid[:, 1:2]
        source = z_here * side + lax.rem(y_here + ry, side)
        wanted = lax.rem(z_here + rz, side) * side + y_here
        npair = pairs.shape[1]
        per_group = npair // (side * side)
        lane = lax.broadcasted_iota(jnp.int32, (grid.shape[0], npair), 1)
        low = source * per_group
        match = (lane >= low) & (lane < low + per_group)
        match = match & (lax.shift_right_logical(pairs[1:2, :], 3) == wanted)
        first = jnp.max(jnp.where(match, pairs[0:1, :] & 7, -1), axis=1, keepdims=True)
        second = jnp.max(jnp.where(match, pairs[1:2, :] & 7, -1), axis=1, keepdims=True)
        column = lax.broadcasted_iota(jnp.int32, (grid.shape[0], BLK), 1)
        tab_vmem[...] = jnp.where(
            column == 0, first, jnp.where(column == 1, second, jnp.where(column == 2, ry, rz))
        )
        copy = pltpu.make_async_copy(tab_vmem, tab, tab_sem)
        copy.start()
        copy.wait()
        lane_tile = lax.broadcasted_iota(jnp.int32, (1, BLK), 1) // rows_x
        for b in range(1, nb):
            for t in range(counts[b]):
                p = base[b - 1] + t
                first = tab[p, 0]
                key = jnp.where(first >= 0, first + BPD * tab[p, 2], -1)
                line = pl.ds(group0[b] + t // per_line, 1)
                held = jnp.full((1, BLK), -1, jnp.int32) if t % per_line == 0 else keys[line, :]
                keys[line, :] = jnp.where(lane_tile == t % per_line, key, held)

    def partial_scores(b):
        if b == 0:
            for k in range(BPD):
                s = dot_tn(own[k], own[k])
                part[b][:, :, k] = s.reshape(2, xs, rows_x, BLK)
            return
        for t, (ry, rz) in enumerate(plan[b - 1]):
            p = base[b - 1] + t
            first = jnp.maximum(tab[p, 0], 0)
            second = jnp.maximum(tab[p, 1], 0)
            s = dot_tn(rowbuf[ry][first], colbuf[rz][second])
            part[b][:, :, t] = s.reshape(2, xs, rows_x, BLK)

    def stage1(b):
        inflight[b] = [
            send(part[b].at[other], from_core[b], c1_send.at[b], c1_recv.at[b], at_core)
        ]

    def x_send(b, i, src, dst, r):
        return send(src, dst, x_sems[0].at[b, i], x_sems[1].at[b, i], at_x(r))

    def stage2(b):
        inflight[b][0].wait_recv()
        part[b][core] = part[b][core] + from_core[b][...]
        inflight[b] = [
            x_send(b, r, part[b].at[core, x_of(r)], from_x[b].at[r - 1], r) for r in range(1, xs)
        ]

    def reduce_rows(b):
        for copy in inflight[b]:
            copy.wait_recv()
        total = part[b][core, x_here]
        for r in range(1, xs):
            total = total + from_x[b][r - 1]
        score[b][core, x_here] = total * scale

    def spread_rows(b):
        mine = score[b].at[core, x_here]
        inflight[b] = [x_send(b, xs + r, mine, mine, r) for r in range(1, xs)]

    def row_partials(b):
        mine = score[b][core, x_here]
        n = counts[b]
        if b == 0:
            row = lax.broadcasted_iota(jnp.int32, mine.shape, 1) + (core * xs + x_here) * rows_x
            values = jnp.where(row == lax.broadcasted_iota(jnp.int32, mine.shape, 2), NEG, mine)
        else:
            values = mine
        top = jnp.max(values, axis=1, keepdims=True)
        total = jnp.sum(jnp.exp(values - top), axis=1, keepdims=True)
        cols = (top + jnp.log(total)).reshape(n, BLK)
        if b == 0:
            diag_stat[...] = cols
            return
        col_stat[pl.ds(base[b - 1], n), :] = cols
        flat = mine.reshape(n * rows_x, BLK)
        for g in range(-(-n // per_line)):
            lines = flat[g * BLK : (g + 1) * BLK]
            if lines.shape[0] < BLK:
                lines = jnp.concatenate([lines, jnp.zeros((BLK - lines.shape[0], BLK), F32)], axis=0)
            row_stat[pl.ds(group0[b] + g, 1), :] = lse_rows(lines.T)

    def stage3(b):
        reduce_rows(b)
        spread_rows(b)
        row_partials(b)

    def stage4(b):
        for copy in inflight[b]:
            copy.wait_recv()
        inflight[b] = [
            send(score[b].at[core], score[b].at[core], c4_send.at[b], c4_recv.at[b], at_core)
        ]

    def stage5(b):
        inflight[b][0].wait_recv()

    def tile(b, t):
        return score[b][:, :, t].reshape(BLK, BLK)

    eye = lax.broadcasted_iota(jnp.int32, (BLK, BLK), 0) == lax.broadcasted_iota(
        jnp.int32, (BLK, BLK), 1
    )

    stages = [stage1, stage2, stage3, stage4, stage5]
    progress = {}

    def tick():
        for b in sorted(progress):
            if progress[b] < len(stages):
                stages[progress[b]](b)
                progress[b] += 1

    for e in range(min(2, events)):
        for f in range(4):
            gather_send(f, e)
    partial_scores(0)
    progress[0] = 0
    tick()
    slot_tables()
    tick()
    for e in range(events):
        for f in range(4):
            gathers[f][e].wait_recv()
            if e + 2 < events:
                gather_send(f, e + 2)
        b = half if e == events - 1 else ((e + 1) // 2 if e % 2 == 1 else 0)
        if b:
            partial_scores(b)
            if b >= half - 1:
                stage1(b)
                stage2(b)
            else:
                progress[b] = 0
        tick()
        tick()
    while any(p < len(stages) for p in progress.values()):
        tick()
    tail = [b for b in (half - 1, half) if b >= 1]
    block_id = lax.broadcasted_iota(jnp.int32, (BPD, BLK), 0)

    def over_lanes(values, combine):
        shift = BLK // 2
        while shift >= rows_x:
            values = combine(values, pltpu.roll(values, shift, 1))
            shift //= 2
        return values

    def col_merge(r, b_from, b_to, more):
        found = list(more)
        for o in range(side):
            if (o, r) in pos and base[b_from] <= pos[(o, r)] < base[b_to]:
                p = pos[(o, r)]
                line = jnp.broadcast_to(col_stat[pl.ds(p, 1), :], (BPD, BLK))
                found.append(jnp.where(block_id == tab[p, 1], line, NEG))
        return merge(found) if found else None

    def row_merge(r, b_from, b_to, more):
        found = []
        for b in range(b_from, b_to):
            for g in range(group0[b + 1], group0[b + 1] + -(-counts[b + 1] // per_line)):
                if all(plan[b][t][0] != r for t in range(counts[b + 1]) if t // per_line == g - group0[b + 1]):
                    continue
                line = jnp.broadcast_to(row_stat[pl.ds(g, 1), :], (BPD, BLK))
                key = jnp.broadcast_to(keys[pl.ds(g, 1), :], (BPD, BLK))
                found.append(jnp.where(key == block_id + BPD * r, line, NEG))
        if not found:
            return merge(more) if more else None
        top = over_lanes(functools.reduce(jnp.maximum, found), jnp.maximum)
        total = functools.reduce(jnp.add, [jnp.exp(v - top) for v in found])
        return merge(list(more) + [top + jnp.log(over_lanes(total, jnp.add))])

    for b in tail:
        if b == half:
            for axis, combine in ((1, col_merge), (0, row_merge)):
                for r in range(side):
                    early = combine(r, 0, half - 1, [])
                    if early is not None:
                        stat_send[axis, r] = early
        reduce_rows(b)
        if b == half:
            for late in reversed(tail):
                spread_rows(late)
        row_partials(b)

    def exchange(step, axis, source, slots):
        return [
            send(
                source(r),
                slots.at[axis, (-r) % side],
                l_send.at[step, axis, r],
                l_recv.at[step, axis, r],
                ahead[axis](r),
            )
            for r in range(1, side)
        ]

    def has_early(axis, r):
        mine = [pos[slot] for slot in pos if slot[1 if axis == 1 else 0] == r]
        return any(p < base[half - 1] for p in mine)

    exchanged = []
    for axis, combine in ((1, col_merge), (0, row_merge)):
        for r in range(side):
            early = [stat_send[axis, r]] if has_early(axis, r) else []
            stat_send[axis, r] = combine(r, half - 1, half, early)
        exchanged += exchange(0, axis, lambda r, axis=axis: stat_send.at[axis, r], stat_recv)
    for copy in exchanged:
        copy.wait_recv()
    dp_stat[0, 0] = merge([stat_send[0, 0]] + [stat_recv[0, r] for r in range(1, side)])
    dp_stat[0, 1] = merge(
        [diag_stat[...], stat_send[1, 0]] + [stat_recv[1, r] for r in range(1, side)]
    )
    exchanged = [
        send(
            dp_stat.at[0],
            dp_stat.at[2 * xs - r],
            dp_sems[0].at[r],
            dp_sems[1].at[r],
            at_dp(r),
        )
        for r in range(1, 2 * xs)
    ]
    for copy in exchanged:
        copy.wait_recv()
    lane_group = lax.broadcasted_iota(jnp.int32, (BPD, BLK), 1) // rows_x
    found = []
    for r in range(2 * xs):
        source = lax.rem(d + r, 2 * xs)
        part_of = lax.rem(source, 2) * xs + lax.div(source, 2)
        found.append(jnp.where(lane_group == part_of, dp_stat[r, 0], NEG))
        found.append(dp_stat[r, 1])
    lse_own = merge(found)
    lse_out[...] = lse_own
    level[0, 0] = lse_own
    level[1, 0] = lse_own
    exchanged = exchange(1, 0, lambda r: level.at[0, 0], level)
    exchanged += exchange(1, 1, lambda r: level.at[1, 0], level)
    stage4(half)
    for copy in exchanged:
        copy.wait_recv()
    stage5(half)

    def two_sided(values, li, lj):
        li = jnp.broadcast_to(li, (BLK, BLK)).T
        return jnp.exp(values - li) + jnp.exp(values - lj)

    def weights(b, start=0, stop=None):
        def body(t, carry):
            p = base[b - 1] + t
            first, second = tab[p, 0], tab[p, 1]
            li = level[0, tab[p, 2], pl.ds(jnp.maximum(first, 0), 1), :]
            lj = level[1, tab[p, 3], pl.ds(jnp.maximum(second, 0), 1), :]
            w = jnp.where(first >= 0, two_sided(tile(b, t), li, lj), 0.0)
            w_ref[p] = w.astype(BF16)
            wt_ref[p] = w.T.astype(BF16)
            return carry

        lax.fori_loop(start, counts[b] if stop is None else stop, body, 0)

    def contribution(axis, rel, c):
        slots = [o for o in range(side) if (rel, o) != (0, 0)]
        for i, o in enumerate(slots):
            p = pos[(rel, o) if axis == 0 else (o, rel)]
            mine, theirs = tab[p, axis], tab[p, 1 - axis]
            lanes = pl.ds(i * BLK, BLK)
            stacked[:, lanes] = bufs[1 - axis][o][jnp.maximum(theirs, 0)]
            w = (wt_ref if axis == 0 else w_ref)[p]
            for k in range(HALF_BPD):
                wide[lanes, pl.ds(k * BLK, BLK)] = jnp.where(
                    mine == c * HALF_BPD + k, w, jnp.zeros_like(w)
                )
        depth = pl.ds(0, len(slots) * BLK)
        return jnp.dot(stacked[:, depth], wide[depth, :], preferred_element_type=F32)

    def by_block(out, offset, values):
        for k in range(HALF_BPD):
            out[offset + k] = values[:, k * BLK : (k + 1) * BLK]

    scatters = [[None] * events for _ in flows]

    def scatter_send(f, e, out):
        axis, sign = flows[f]
        scatters[f][e] = send(
            out, ring_in[f][e], rs_send.at[f, e], rs_recv.at[f, e], ahead[axis](sign % side)
        )

    for e in range(events):
        rho = half - (e + 1) // 2
        if e % 2 == 1:
            if rho == half - 1:
                stage4(rho)
                stage5(rho)
            weights(rho)
        for f, (axis, sign) in enumerate(flows):
            if e == 0 and sign > 0:
                weights(half, side * axis, side if axis == 0 else None)
            own_part = contribution(axis, (rho * sign) % side, chunk_of(sign, e))
            if e < 2:
                by_block(fresh.at[f, e], 0, own_part.astype(BF16))
                scatter_send(f, e, fresh.at[f, e])
            else:
                by_block(temp.at[f], 0, own_part)
        if e >= 2:
            for f in range(4):
                scatters[f][e - 2].wait_recv()
                out = ring_in[f][e - 2]
                out[...] = (temp[f] + out[...].astype(F32)).astype(BF16)
                scatter_send(f, e, out)

    for k in range(BPD):
        line = lse_own[k : k + 1]
        values = jnp.where(eye, NEG, tile(0, k))
        w = two_sided(values, line, line).T.astype(BF16)
        swap = lax.broadcasted_iota(jnp.int32, (BLK, BLK), 0) == partner[pl.ds(k, 1), :]
        swap = jnp.where(swap, 1.0, 0.0).astype(BF16)
        acc[k] = jnp.dot(own[k], w, preferred_element_type=F32) - 2.0 * jnp.dot(
            own[k], swap, preferred_element_type=F32
        )
    for axis in (0, 1):
        for c in (0, 1):
            rows = pl.ds(c * HALF_BPD, HALF_BPD)
            by_block(temp.at[0], 0, contribution(axis, 0, c))
            acc[rows] = acc[rows] + temp[0]
    last = [e for e in range(events) if half - (e + 1) // 2 == 1]
    for e in last[:-1]:
        for f, (axis, sign) in enumerate(flows):
            scatters[f][e].wait_recv()
            rows = pl.ds(chunk_of(sign, e) * HALF_BPD, HALF_BPD)
            acc[rows] = acc[rows] + ring_in[f][e][...].astype(F32)
    stores = []
    e = last[-1]
    for sign in (1, -1):
        pair = [f for f in range(4) if flows[f][1] == sign]
        for f in pair:
            scatters[f][e].wait_recv()
        for i in range(HALF_BPD):
            k = chunk_of(sign, e) * HALF_BPD + i
            total = acc[k]
            for f in pair:
                total = total + ring_in[f][e][i].astype(F32)
            done[k] = total.astype(BF16)
            stores.append(
                pltpu.make_async_copy(
                    done.at[k], grad_out.at[:, pl.ds(k * BLK, BLK)], out_sem.at[k]
                )
            )
            stores[-1].start()
    for copy in stores:
        copy.wait()
    for copy in started:
        copy.wait_send()


def fused(embeddings, pairs, partner, side, xs):
    width = embeddings.shape[0]
    half = side // 2
    plan = slot_plan(side)
    counts = [BPD] + [len(batch) for batch in plan]
    nb = len(counts)
    nslot = sum(counts[1:])
    events = 2 * half - 1
    rows_x = BLK // (2 * xs)
    dma = pltpu.SemaphoreType.DMA
    blocks = pltpu.VMEM((BPD, width, BLK), BF16)
    chunk = pltpu.VMEM((HALF_BPD, width, BLK), BF16)
    stats = pltpu.VMEM((2, side, BPD, BLK), F32)
    scratch = [blocks] * (2 * side - 1)
    scratch += [pltpu.VMEM((2, xs, n, rows_x, BLK), F32) for n in counts]
    scratch += [pltpu.VMEM((xs, n, rows_x, BLK), F32) for n in counts]
    scratch += [pltpu.VMEM((xs - 1, n, rows_x, BLK), F32) for n in counts]
    scratch += [pltpu.VMEM((2, xs, n, rows_x, BLK), F32) for n in counts]
    padded = -(-nslot // 8) * 8
    scratch += [pltpu.VMEM((padded, BLK), F32)] * 2 + [pltpu.VMEM((BPD, BLK), F32)]
    scratch += [stats] * 3 + [pltpu.VMEM((nslot, BLK, BLK), BF16)] * 2
    scratch += [pltpu.VMEM((padded, BLK), jnp.int32), pltpu.VMEM((2 * xs, 2, BPD, BLK), F32)]
    scratch += [
        pltpu.VMEM((side * BLK, HALF_BPD * BLK), BF16),
        pltpu.VMEM((width, side * BLK), BF16),
        pltpu.VMEM((4, HALF_BPD, width, BLK), F32),
        pltpu.VMEM((BPD, width, BLK), F32),
        pltpu.VMEM((4, 2, HALF_BPD, width, BLK), BF16),
        blocks,
        pltpu.VMEM((padded, BLK), jnp.int32),
        pltpu.SMEM((padded, BLK), jnp.int32),
    ]
    scratch += [chunk] * (4 * events)
    scratch += [dma((4, events))] * 2 + [dma((nb,))] * 2 + [dma((nb, 2 * xs))] * 2
    scratch += [dma((nb,))] * 2 + [dma((2, 2, side))] * 2 + [dma((4, events))] * 2
    scratch += [dma((BPD,))] * 2 + [dma(())] + [dma((2 * xs,))] * 2
    anywhere = pl.BlockSpec(memory_space=pl.ANY)
    vmem = pl.BlockSpec(memory_space=pltpu.VMEM)
    flops = 2 * BLK * BLK * width * (counts[0] * 4 + nslot * (1 + 2 * BPD))
    return pl.pallas_call(
        functools.partial(kernel, side, xs, 2.0 / math.sqrt(D)),
        out_shape=(
            jax.ShapeDtypeStruct((BPD, BLK), F32),
            jax.ShapeDtypeStruct((width, BPD * BLK), BF16),
        ),
        in_specs=[anywhere, vmem, vmem, vmem],
        out_specs=(vmem, anywhere),
        scratch_shapes=scratch,
        compiler_params=pltpu.CompilerParams(
            collective_id=0, has_side_effects=True, vmem_limit_bytes=VMEM_BYTES
        ),
        cost_estimate=pl.CostEstimate(
            flops=flops, bytes_accessed=4 * embeddings.size, transcendentals=6 * nslot * BLK * BLK
        ),
    )(embeddings, pairs, partner, jnp.asarray(slot_grid(side)))


def per_device(embeddings, pairs, partner):
    rows_here, width = embeddings.shape
    side = math.isqrt(lax.axis_size("tensor"))
    xs = lax.axis_size("dp") // 2
    lse, grad = fused(
        embeddings.T, pairs.T, (partner % BLK).reshape(BPD, BLK), side, xs
    )
    return lse.reshape(rows_here), grad.T


def solution(mesh):
    in_specs = (P("tensor", "dp"), P(), P("tensor"))
    out_specs = (P("tensor"), P("tensor", "dp"))
    return jax.shard_map(
        per_device, mesh=mesh, in_specs=in_specs, out_specs=out_specs, check_vma=False
    )
```

```python
import functools
import math

import jax
import jax.numpy as jnp
import numpy as np
from jax import lax
from jax.experimental import pallas as pl
from jax.experimental.pallas import tpu as pltpu
from jax.sharding import PartitionSpec as P

D = 3584
BPD = 8
BLK = 128
HALF_BPD = BPD // 2
NEG = -1e30
VMEM_BYTES = 63 * 1024 * 1024
MESH = pl.DeviceIdType.MESH
F32 = jnp.float32
BF16 = jnp.bfloat16


def ring_distance(rel, side):
    return min(rel, side - rel)


def slot_plan(side):
    batches = []
    for step in range(1, side // 2 + 1):
        batch = [
            (ry, rz)
            for ry in range(side)
            for rz in range(side)
            if max(ring_distance(ry, side), ring_distance(rz, side)) == step
        ]
        batches.append(sorted(batch, key=lambda slot: slot[0] != side // 2))
    return batches


def slot_grid(side):
    order = [slot for batch in slot_plan(side) for slot in batch]
    grid = np.zeros((-(-len(order) // 8) * 8, BLK), np.int32)
    grid[: len(order), :2] = order
    return grid


def lse_rows(values):
    top = jnp.max(values, axis=0, keepdims=True)
    return top + jnp.log(jnp.sum(jnp.exp(values - top), axis=0, keepdims=True))


def merge(parts):
    top = functools.reduce(jnp.maximum, parts)
    return top + jnp.log(functools.reduce(jnp.add, [jnp.exp(p - top) for p in parts]))


def kernel(side, xs, scale, *refs):
    half = side // 2
    plan = slot_plan(side)
    counts = [BPD] + [len(batch) for batch in plan]
    nb = len(counts)
    pos = {slot: i for i, slot in enumerate(s for batch in plan for s in batch)}
    base = [0]
    for batch in plan:
        base.append(base[-1] + len(batch))
    events = 2 * half - 1

    refs = list(refs)

    def take(n):
        out = refs[:n]
        del refs[:n]
        return out

    emb, pairs, partner, grid, lse_out, grad_out = take(6)
    (own,) = take(1)
    rowbuf = [own] + take(side - 1)
    colbuf = [own] + take(side - 1)
    part = take(nb)
    from_core = take(nb)
    from_x = take(nb)
    score = take(nb)
    (row_stat, col_stat, diag_stat, stat_send, stat_recv, level, w_ref, wt_ref) = take(8)
    (keys, dp_stat) = take(2)
    (wide, stacked, temp, acc, fresh, done, tab_vmem, tab) = take(8)
    ring_in = [take(events) for _ in range(4)]
    (ag_send, ag_recv, c1_send, c1_recv) = take(4)
    x_sems = take(2)
    (c4_send, c4_recv, l_send, l_recv, rs_send, rs_recv, in_sem, out_sem, tab_sem) = take(9)
    dp_sems = take(2)

    me = lax.axis_index("tensor")
    d = lax.axis_index("dp")
    z_here, y_here = lax.div(me, side), lax.rem(me, side)
    x_here, core = lax.div(d, 2), lax.rem(d, 2)
    other = 1 - core

    def at_y(r):
        return {"dp": d, "tensor": z_here * side + lax.rem(y_here + r, side)}

    def at_z(r):
        return {"dp": d, "tensor": lax.rem(z_here + r, side) * side + y_here}

    def x_of(r):
        return lax.rem(x_here + r + xs, xs)

    def at_x(r):
        return {"dp": x_of(r) * 2 + core, "tensor": me}

    def at_dp(r):
        return {"dp": lax.rem(d + r, 2 * xs), "tensor": me}

    at_core = {"dp": x_here * 2 + other, "tensor": me}
    peers = [at_y(r) for r in range(1, side)] + [at_z(r) for r in range(1, side)]
    peers += [at_dp(r) for r in range(1, 2 * xs)]
    loads = [
        pltpu.make_async_copy(emb.at[:, pl.ds(k * BLK, BLK)], own.at[k], in_sem.at[k])
        for k in range(BPD)
    ]
    for copy in loads:
        copy.start()
    barrier = pltpu.get_barrier_semaphore()
    for peer in peers:
        pl.semaphore_signal(barrier, inc=1, device_id=peer, device_id_type=MESH)
    for copy in loads:
        copy.wait()
    pl.semaphore_wait(barrier, len(peers))

    started = []

    def send(src, dst, send_sem, recv_sem, device):
        copy = pltpu.make_async_remote_copy(
            src_ref=src,
            dst_ref=dst,
            send_sem=send_sem,
            recv_sem=recv_sem,
            device_id=device,
            device_id_type=MESH,
        )
        copy.start()
        started.append(copy)
        return copy

    flows = [(0, 1), (0, -1), (1, 1), (1, -1)]
    bufs = [rowbuf, colbuf]
    ahead = [at_y, at_z]

    def chunk_of(sign, e):
        first = 0 if sign > 0 else 1
        return first if e % 2 == 0 else 1 - first

    def chunk(ref, c):
        return ref.at[pl.ds(c * HALF_BPD, HALF_BPD)]

    gathers = [[None] * events for _ in flows]

    def gather_send(f, e):
        axis, sign = flows[f]
        s, c = e // 2, chunk_of(sign, e)
        gathers[f][e] = send(
            chunk(bufs[axis][(-s * sign) % side], c),
            chunk(bufs[axis][(-(s + 1) * sign) % side], c),
            ag_send.at[f, e],
            ag_recv.at[f, e],
            ahead[axis](sign % side),
        )

    inflight = {}
    rows_x = BLK // (2 * xs)
    per_line = BLK // rows_x
    group0 = [0, 0]
    for n in counts[1:]:
        group0.append(group0[-1] + -(-n // per_line))

    def dot_tn(a, b):
        return lax.dot_general(a, b, (((0,), (0,)), ((), ())), preferred_element_type=F32)

    def slot_tables():
        ry, rz = grid[:, 0:1], grid[:, 1:2]
        source = z_here * side + lax.rem(y_here + ry, side)
        wanted = lax.rem(z_here + rz, side) * side + y_here
        npair = pairs.shape[1]
        per_group = npair // (side * side)
        lane = lax.broadcasted_iota(jnp.int32, (grid.shape[0], npair), 1)
        low = source * per_group
        match = (lane >= low) & (lane < low + per_group)
        match = match & (lax.shift_right_logical(pairs[1:2, :], 3) == wanted)
        first = jnp.max(jnp.where(match, pairs[0:1, :] & 7, -1), axis=1, keepdims=True)
        second = jnp.max(jnp.where(match, pairs[1:2, :] & 7, -1), axis=1, keepdims=True)
        column = lax.broadcasted_iota(jnp.int32, (grid.shape[0], BLK), 1)
        tab_vmem[...] = jnp.where(
            column == 0, first, jnp.where(column == 1, second, jnp.where(column == 2, ry, rz))
        )
        copy = pltpu.make_async_copy(tab_vmem, tab, tab_sem)
        copy.start()
        copy.wait()
        lane_tile = lax.broadcasted_iota(jnp.int32, (1, BLK), 1) // rows_x
        for b in range(1, nb):
            for t in range(counts[b]):
                p = base[b - 1] + t
                first = tab[p, 0]
                key = jnp.where(first >= 0, first + BPD * tab[p, 2], -1)
                line = pl.ds(group0[b] + t // per_line, 1)
                held = jnp.full((1, BLK), -1, jnp.int32) if t % per_line == 0 else keys[line, :]
                keys[line, :] = jnp.where(lane_tile == t % per_line, key, held)

    def partial_scores(b):
        if b == 0:
            for k in range(BPD):
                s = dot_tn(own[k], own[k])
                part[b][:, :, k] = s.reshape(2, xs, rows_x, BLK)
            return
        for t, (ry, rz) in enumerate(plan[b - 1]):
            p = base[b - 1] + t
            first = jnp.maximum(tab[p, 0], 0)
            second = jnp.maximum(tab[p, 1], 0)
            s = dot_tn(rowbuf[ry][first], colbuf[rz][second])
            part[b][:, :, t] = s.reshape(2, xs, rows_x, BLK)

    def stage1(b):
        inflight[b] = [
            send(part[b].at[other], from_core[b], c1_send.at[b], c1_recv.at[b], at_core)
        ]

    def x_send(b, i, src, dst, r):
        return send(src, dst, x_sems[0].at[b, i], x_sems[1].at[b, i], at_x(r))

    def stage2(b):
        inflight[b][0].wait_recv()
        part[b][core] = part[b][core] + from_core[b][...]
        inflight[b] = [
            x_send(b, r, part[b].at[core, x_of(r)], from_x[b].at[r - 1], r) for r in range(1, xs)
        ]

    def reduce_rows(b):
        for copy in inflight[b]:
            copy.wait_recv()
        total = part[b][core, x_here]
        for r in range(1, xs):
            total = total + from_x[b][r - 1]
        score[b][core, x_here] = total * scale

    def spread_rows(b):
        mine = score[b].at[core, x_here]
        inflight[b] = [x_send(b, xs + r, mine, mine, r) for r in range(1, xs)]

    def row_partials(b):
        mine = score[b][core, x_here]
        n = counts[b]
        if b == 0:
            row = lax.broadcasted_iota(jnp.int32, mine.shape, 1) + (core * xs + x_here) * rows_x
            values = jnp.where(row == lax.broadcasted_iota(jnp.int32, mine.shape, 2), NEG, mine)
        else:
            values = mine
        top = jnp.max(values, axis=1, keepdims=True)
        total = jnp.sum(jnp.exp(values - top), axis=1, keepdims=True)
        cols = (top + jnp.log(total)).reshape(n, BLK)
        if b == 0:
            diag_stat[...] = cols
            return
        col_stat[pl.ds(base[b - 1], n), :] = cols
        flat = mine.reshape(n * rows_x, BLK)
        for g in range(-(-n // per_line)):
            lines = flat[g * BLK : (g + 1) * BLK]
            if lines.shape[0] < BLK:
                lines = jnp.concatenate([lines, jnp.zeros((BLK - lines.shape[0], BLK), F32)], axis=0)
            row_stat[pl.ds(group0[b] + g, 1), :] = lse_rows(lines.T)

    def stage3(b):
        reduce_rows(b)
        spread_rows(b)
        row_partials(b)

    def stage4(b):
        for copy in inflight[b]:
            copy.wait_recv()
        inflight[b] = [
            send(score[b].at[core], score[b].at[core], c4_send.at[b], c4_recv.at[b], at_core)
        ]

    def stage5(b):
        inflight[b][0].wait_recv()

    def tile(b, t):
        return score[b][:, :, t].reshape(BLK, BLK)

    eye = lax.broadcasted_iota(jnp.int32, (BLK, BLK), 0) == lax.broadcasted_iota(
        jnp.int32, (BLK, BLK), 1
    )

    stages = [stage1, stage2, stage3, stage4, stage5]
    progress = {}

    def tick():
        for b in sorted(progress):
            if progress[b] < len(stages):
                stages[progress[b]](b)
                progress[b] += 1

    for e in range(min(2, events)):
        for f in range(4):
            gather_send(f, e)
    partial_scores(0)
    progress[0] = 0
    tick()
    slot_tables()
    tick()
    for e in range(events):
        for f in range(4):
            gathers[f][e].wait_recv()
            if e + 2 < events:
                gather_send(f, e + 2)
        b = half if e == events - 1 else ((e + 1) // 2 if e % 2 == 1 else 0)
        if b:
            partial_scores(b)
            if b >= half - 1:
                stage1(b)
                stage2(b)
            else:
                progress[b] = 0
        tick()
        tick()
    while any(p < len(stages) for p in progress.values()):
        tick()
    tail = [b for b in (half - 1, half) if b >= 1]
    block_id = lax.broadcasted_iota(jnp.int32, (BPD, BLK), 0)

    def over_lanes(values, combine):
        shift = BLK // 2
        while shift >= rows_x:
            values = combine(values, pltpu.roll(values, shift, 1))
            shift //= 2
        return values

    def col_merge(r, b_from, b_to, more):
        found = list(more)
        for o in range(side):
            if (o, r) in pos and base[b_from] <= pos[(o, r)] < base[b_to]:
                p = pos[(o, r)]
                line = jnp.broadcast_to(col_stat[pl.ds(p, 1), :], (BPD, BLK))
                found.append(jnp.where(block_id == tab[p, 1], line, NEG))
        return merge(found) if found else None

    def row_merge(r, b_from, b_to, more):
        found = []
        for b in range(b_from, b_to):
            for g in range(group0[b + 1], group0[b + 1] + -(-counts[b + 1] // per_line)):
                if all(plan[b][t][0] != r for t in range(counts[b + 1]) if t // per_line == g - group0[b + 1]):
                    continue
                line = jnp.broadcast_to(row_stat[pl.ds(g, 1), :], (BPD, BLK))
                key = jnp.broadcast_to(keys[pl.ds(g, 1), :], (BPD, BLK))
                found.append(jnp.where(key == block_id + BPD * r, line, NEG))
        if not found:
            return merge(more) if more else None
        top = over_lanes(functools.reduce(jnp.maximum, found), jnp.maximum)
        total = functools.reduce(jnp.add, [jnp.exp(v - top) for v in found])
        return merge(list(more) + [top + jnp.log(over_lanes(total, jnp.add))])

    for b in tail:
        if b == half:
            for axis, combine in ((1, col_merge), (0, row_merge)):
                for r in range(side):
                    early = combine(r, 0, half - 1, [])
                    if early is not None:
                        stat_send[axis, r] = early
        reduce_rows(b)
        if b == half:
            spread_rows(b)
        row_partials(b)

    def exchange(step, axis, source, slots):
        return [
            send(
                source(r),
                slots.at[axis, (-r) % side],
                l_send.at[step, axis, r],
                l_recv.at[step, axis, r],
                ahead[axis](r),
            )
            for r in range(1, side)
        ]

    def has_early(axis, r):
        mine = [pos[slot] for slot in pos if slot[1 if axis == 1 else 0] == r]
        return any(p < base[half - 1] for p in mine)

    exchanged = []
    for axis, combine in ((1, col_merge), (0, row_merge)):
        for r in range(side):
            early = [stat_send[axis, r]] if has_early(axis, r) else []
            stat_send[axis, r] = combine(r, half - 1, half, early)
        exchanged += exchange(0, axis, lambda r, axis=axis: stat_send.at[axis, r], stat_recv)
    for copy in exchanged:
        copy.wait_recv()
    dp_stat[0, 0] = merge([stat_send[0, 0]] + [stat_recv[0, r] for r in range(1, side)])
    dp_stat[0, 1] = merge(
        [diag_stat[...], stat_send[1, 0]] + [stat_recv[1, r] for r in range(1, side)]
    )
    exchanged = [
        send(
            dp_stat.at[0],
            dp_stat.at[2 * xs - r],
            dp_sems[0].at[r],
            dp_sems[1].at[r],
            at_dp(r),
        )
        for r in range(1, 2 * xs)
    ]
    for b in tail[:-1]:
        spread_rows(b)
    for copy in exchanged:
        copy.wait_recv()
    lane_group = lax.broadcasted_iota(jnp.int32, (BPD, BLK), 1) // rows_x
    found = []
    for r in range(2 * xs):
        source = lax.rem(d + r, 2 * xs)
        part_of = lax.rem(source, 2) * xs + lax.div(source, 2)
        found.append(jnp.where(lane_group == part_of, dp_stat[r, 0], NEG))
        found.append(dp_stat[r, 1])
    lse_own = merge(found)
    lse_out[...] = lse_own
    level[0, 0] = lse_own
    level[1, 0] = lse_own
    exchanged = exchange(1, 0, lambda r: level.at[0, 0], level)
    exchanged += exchange(1, 1, lambda r: level.at[1, 0], level)
    stage4(half)
    for copy in exchanged:
        copy.wait_recv()
    stage5(half)

    def two_sided(values, li, lj):
        li = jnp.broadcast_to(li, (BLK, BLK)).T
        return jnp.exp(values - li) + jnp.exp(values - lj)

    def weights(b, start=0, stop=None):
        def body(t, carry):
            p = base[b - 1] + t
            first, second = tab[p, 0], tab[p, 1]
            li = level[0, tab[p, 2], pl.ds(jnp.maximum(first, 0), 1), :]
            lj = level[1, tab[p, 3], pl.ds(jnp.maximum(second, 0), 1), :]
            w = jnp.where(first >= 0, two_sided(tile(b, t), li, lj), 0.0)
            w_ref[p] = w.astype(BF16)
            wt_ref[p] = w.T.astype(BF16)
            return carry

        lax.fori_loop(start, counts[b] if stop is None else stop, body, 0)

    def contribution(axis, rel, c):
        slots = [o for o in range(side) if (rel, o) != (0, 0)]
        for i, o in enumerate(slots):
            p = pos[(rel, o) if axis == 0 else (o, rel)]
            mine, theirs = tab[p, axis], tab[p, 1 - axis]
            lanes = pl.ds(i * BLK, BLK)
            stacked[:, lanes] = bufs[1 - axis][o][jnp.maximum(theirs, 0)]
            w = (wt_ref if axis == 0 else w_ref)[p]
            for k in range(HALF_BPD):
                wide[lanes, pl.ds(k * BLK, BLK)] = jnp.where(
                    mine == c * HALF_BPD + k, w, jnp.zeros_like(w)
                )
        depth = pl.ds(0, len(slots) * BLK)
        return jnp.dot(stacked[:, depth], wide[depth, :], preferred_element_type=F32)

    def by_block(out, offset, values):
        for k in range(HALF_BPD):
            out[offset + k] = values[:, k * BLK : (k + 1) * BLK]

    scatters = [[None] * events for _ in flows]

    def scatter_send(f, e, out):
        axis, sign = flows[f]
        scatters[f][e] = send(
            out, ring_in[f][e], rs_send.at[f, e], rs_recv.at[f, e], ahead[axis](sign % side)
        )

    for e in range(events):
        rho = half - (e + 1) // 2
        if e % 2 == 1:
            if rho == half - 1:
                stage4(rho)
                stage5(rho)
            weights(rho)
        for f, (axis, sign) in enumerate(flows):
            if e == 0 and sign > 0:
                weights(half, side * axis, side if axis == 0 else None)
            own_part = contribution(axis, (rho * sign) % side, chunk_of(sign, e))
            if e < 2:
                by_block(fresh.at[f, e], 0, own_part.astype(BF16))
                scatter_send(f, e, fresh.at[f, e])
            else:
                by_block(temp.at[f], 0, own_part)
        if e >= 2:
            for f in range(4):
                scatters[f][e - 2].wait_recv()
                out = ring_in[f][e - 2]
                out[...] = (temp[f] + out[...].astype(F32)).astype(BF16)
                scatter_send(f, e, out)

    for k in range(BPD):
        line = lse_own[k : k + 1]
        values = jnp.where(eye, NEG, tile(0, k))
        w = two_sided(values, line, line).T.astype(BF16)
        swap = lax.broadcasted_iota(jnp.int32, (BLK, BLK), 0) == partner[pl.ds(k, 1), :]
        swap = jnp.where(swap, 1.0, 0.0).astype(BF16)
        acc[k] = jnp.dot(own[k], w, preferred_element_type=F32) - 2.0 * jnp.dot(
            own[k], swap, preferred_element_type=F32
        )
    for axis in (0, 1):
        for c in (0, 1):
            rows = pl.ds(c * HALF_BPD, HALF_BPD)
            by_block(temp.at[0], 0, contribution(axis, 0, c))
            acc[rows] = acc[rows] + temp[0]
    last = [e for e in range(events) if half - (e + 1) // 2 == 1]
    for e in last[:-1]:
        for f, (axis, sign) in enumerate(flows):
            scatters[f][e].wait_recv()
            rows = pl.ds(chunk_of(sign, e) * HALF_BPD, HALF_BPD)
            acc[rows] = acc[rows] + ring_in[f][e][...].astype(F32)
    stores = []
    e = last[-1]
    for sign in (1, -1):
        pair = [f for f in range(4) if flows[f][1] == sign]
        for f in pair:
            scatters[f][e].wait_recv()
        for i in range(HALF_BPD):
            k = chunk_of(sign, e) * HALF_BPD + i
            total = acc[k]
            for f in pair:
                total = total + ring_in[f][e][i].astype(F32)
            done[k] = total.astype(BF16)
            stores.append(
                pltpu.make_async_copy(
                    done.at[k], grad_out.at[:, pl.ds(k * BLK, BLK)], out_sem.at[k]
                )
            )
            stores[-1].start()
    for copy in stores:
        copy.wait()
    for copy in started:
        copy.wait_send()


def fused(embeddings, pairs, partner, side, xs):
    width = embeddings.shape[0]
    half = side // 2
    plan = slot_plan(side)
    counts = [BPD] + [len(batch) for batch in plan]
    nb = len(counts)
    nslot = sum(counts[1:])
    events = 2 * half - 1
    rows_x = BLK // (2 * xs)
    dma = pltpu.SemaphoreType.DMA
    blocks = pltpu.VMEM((BPD, width, BLK), BF16)
    chunk = pltpu.VMEM((HALF_BPD, width, BLK), BF16)
    stats = pltpu.VMEM((2, side, BPD, BLK), F32)
    scratch = [blocks] * (2 * side - 1)
    scratch += [pltpu.VMEM((2, xs, n, rows_x, BLK), F32) for n in counts]
    scratch += [pltpu.VMEM((xs, n, rows_x, BLK), F32) for n in counts]
    scratch += [pltpu.VMEM((xs - 1, n, rows_x, BLK), F32) for n in counts]
    scratch += [pltpu.VMEM((2, xs, n, rows_x, BLK), F32) for n in counts]
    padded = -(-nslot // 8) * 8
    scratch += [pltpu.VMEM((padded, BLK), F32)] * 2 + [pltpu.VMEM((BPD, BLK), F32)]
    scratch += [stats] * 3 + [pltpu.VMEM((nslot, BLK, BLK), BF16)] * 2
    scratch += [pltpu.VMEM((padded, BLK), jnp.int32), pltpu.VMEM((2 * xs, 2, BPD, BLK), F32)]
    scratch += [
        pltpu.VMEM((side * BLK, HALF_BPD * BLK), BF16),
        pltpu.VMEM((width, side * BLK), BF16),
        pltpu.VMEM((4, HALF_BPD, width, BLK), F32),
        pltpu.VMEM((BPD, width, BLK), F32),
        pltpu.VMEM((4, 2, HALF_BPD, width, BLK), BF16),
        blocks,
        pltpu.VMEM((padded, BLK), jnp.int32),
        pltpu.SMEM((padded, BLK), jnp.int32),
    ]
    scratch += [chunk] * (4 * events)
    scratch += [dma((4, events))] * 2 + [dma((nb,))] * 2 + [dma((nb, 2 * xs))] * 2
    scratch += [dma((nb,))] * 2 + [dma((2, 2, side))] * 2 + [dma((4, events))] * 2
    scratch += [dma((BPD,))] * 2 + [dma(())] + [dma((2 * xs,))] * 2
    anywhere = pl.BlockSpec(memory_space=pl.ANY)
    vmem = pl.BlockSpec(memory_space=pltpu.VMEM)
    flops = 2 * BLK * BLK * width * (counts[0] * 4 + nslot * (1 + 2 * BPD))
    return pl.pallas_call(
        functools.partial(kernel, side, xs, 2.0 / math.sqrt(D)),
        out_shape=(
            jax.ShapeDtypeStruct((BPD, BLK), F32),
            jax.ShapeDtypeStruct((width, BPD * BLK), BF16),
        ),
        in_specs=[anywhere, vmem, vmem, vmem],
        out_specs=(vmem, anywhere),
        scratch_shapes=scratch,
        compiler_params=pltpu.CompilerParams(
            collective_id=0, has_side_effects=True, vmem_limit_bytes=VMEM_BYTES
        ),
        cost_estimate=pl.CostEstimate(
            flops=flops, bytes_accessed=4 * embeddings.size, transcendentals=6 * nslot * BLK * BLK
        ),
    )(embeddings, pairs, partner, jnp.asarray(slot_grid(side)))


def per_device(embeddings, pairs, partner):
    rows_here, width = embeddings.shape
    side = math.isqrt(lax.axis_size("tensor"))
    xs = lax.axis_size("dp") // 2
    lse, grad = fused(
        embeddings.T, pairs.T, (partner % BLK).reshape(BPD, BLK), side, xs
    )
    return lse.reshape(rows_here), grad.T


def solution(mesh):
    in_specs = (P("tensor", "dp"), P(), P("tensor"))
    out_specs = (P("tensor"), P("tensor", "dp"))
    return jax.shard_map(
        per_device, mesh=mesh, in_specs=in_specs, out_specs=out_specs, check_vma=False
    )
```

```python
import functools
import math

import jax
import jax.numpy as jnp
import numpy as np
from jax import lax
from jax.experimental import pallas as pl
from jax.experimental.pallas import tpu as pltpu
from jax.sharding import PartitionSpec as P

D = 3584
BPD = 8
BLK = 128
HALF_BPD = BPD // 2
NEG = -1e30
VMEM_BYTES = 63 * 1024 * 1024
MESH = pl.DeviceIdType.MESH
F32 = jnp.float32
BF16 = jnp.bfloat16


def ring_distance(rel, side):
    return min(rel, side - rel)


def slot_plan(side):
    batches = []
    for step in range(1, side // 2 + 1):
        batch = [
            (ry, rz)
            for ry in range(side)
            for rz in range(side)
            if max(ring_distance(ry, side), ring_distance(rz, side)) == step
        ]
        batches.append(sorted(batch, key=lambda slot: slot[0] != side // 2))
    return batches


def slot_grid(side):
    order = [slot for batch in slot_plan(side) for slot in batch]
    grid = np.zeros((-(-len(order) // 8) * 8, BLK), np.int32)
    grid[: len(order), :2] = order
    return grid


def lse_rows(values):
    top = jnp.max(values, axis=0, keepdims=True)
    return top + jnp.log(jnp.sum(jnp.exp(values - top), axis=0, keepdims=True))


def merge(parts):
    top = functools.reduce(jnp.maximum, parts)
    return top + jnp.log(functools.reduce(jnp.add, [jnp.exp(p - top) for p in parts]))


def kernel(side, xs, scale, *refs):
    half = side // 2
    plan = slot_plan(side)
    counts = [BPD] + [len(batch) for batch in plan]
    nb = len(counts)
    pos = {slot: i for i, slot in enumerate(s for batch in plan for s in batch)}
    base = [0]
    for batch in plan:
        base.append(base[-1] + len(batch))
    events = 2 * half - 1

    refs = list(refs)

    def take(n):
        out = refs[:n]
        del refs[:n]
        return out

    emb, pairs, partner, grid, lse_out, grad_out = take(6)
    (own,) = take(1)
    rowbuf = [own] + take(side - 1)
    colbuf = [own] + take(side - 1)
    part = take(nb)
    from_core = take(nb)
    from_x = take(nb)
    score = take(nb)
    (row_stat, col_stat, diag_stat, stat_send, stat_recv, level, w_ref, wt_ref) = take(8)
    (keys, dp_stat) = take(2)
    (wide, stacked, temp, acc, fresh, done, tab_vmem, tab) = take(8)
    ring_in = [take(events) for _ in range(4)]
    (ag_send, ag_recv, c1_send, c1_recv) = take(4)
    x_sems = take(2)
    (c4_send, c4_recv, l_send, l_recv, rs_send, rs_recv, in_sem, out_sem, tab_sem) = take(9)
    dp_sems = take(2)

    me = lax.axis_index("tensor")
    d = lax.axis_index("dp")
    z_here, y_here = lax.div(me, side), lax.rem(me, side)
    x_here, core = lax.div(d, 2), lax.rem(d, 2)
    other = 1 - core

    def at_y(r):
        return {"dp": d, "tensor": z_here * side + lax.rem(y_here + r, side)}

    def at_z(r):
        return {"dp": d, "tensor": lax.rem(z_here + r, side) * side + y_here}

    def x_of(r):
        return lax.rem(x_here + r + xs, xs)

    def at_x(r):
        return {"dp": x_of(r) * 2 + core, "tensor": me}

    def at_dp(r):
        return {"dp": lax.rem(d + r, 2 * xs), "tensor": me}

    at_core = {"dp": x_here * 2 + other, "tensor": me}
    peers = [at_y(r) for r in range(1, side)] + [at_z(r) for r in range(1, side)]
    peers += [at_dp(r) for r in range(1, 2 * xs)]
    loads = [
        pltpu.make_async_copy(emb.at[:, pl.ds(k * BLK, BLK)], own.at[k], in_sem.at[k])
        for k in range(BPD)
    ]
    for copy in loads:
        copy.start()
    barrier = pltpu.get_barrier_semaphore()
    for peer in peers:
        pl.semaphore_signal(barrier, inc=1, device_id=peer, device_id_type=MESH)
    for copy in loads:
        copy.wait()
    pl.semaphore_wait(barrier, len(peers))

    started = []

    def send(src, dst, send_sem, recv_sem, device):
        copy = pltpu.make_async_remote_copy(
            src_ref=src,
            dst_ref=dst,
            send_sem=send_sem,
            recv_sem=recv_sem,
            device_id=device,
            device_id_type=MESH,
        )
        copy.start()
        started.append(copy)
        return copy

    flows = [(0, 1), (0, -1), (1, 1), (1, -1)]
    bufs = [rowbuf, colbuf]
    ahead = [at_y, at_z]

    def chunk_of(sign, e):
        first = 0 if sign > 0 else 1
        return first if e % 2 == 0 else 1 - first

    def chunk(ref, c):
        return ref.at[pl.ds(c * HALF_BPD, HALF_BPD)]

    gathers = [[None] * events for _ in flows]

    def gather_send(f, e):
        axis, sign = flows[f]
        s, c = e // 2, chunk_of(sign, e)
        gathers[f][e] = send(
            chunk(bufs[axis][(-s * sign) % side], c),
            chunk(bufs[axis][(-(s + 1) * sign) % side], c),
            ag_send.at[f, e],
            ag_recv.at[f, e],
            ahead[axis](sign % side),
        )

    inflight = {}
    rows_x = BLK // (2 * xs)
    per_line = BLK // rows_x
    group0 = [0, 0]
    for n in counts[1:]:
        group0.append(group0[-1] + -(-n // per_line))

    def dot_tn(a, b):
        return lax.dot_general(a, b, (((0,), (0,)), ((), ())), preferred_element_type=F32)

    def slot_tables():
        ry, rz = grid[:, 0:1], grid[:, 1:2]
        source = z_here * side + lax.rem(y_here + ry, side)
        wanted = lax.rem(z_here + rz, side) * side + y_here
        npair = pairs.shape[1]
        per_group = npair // (side * side)
        lane = lax.broadcasted_iota(jnp.int32, (grid.shape[0], npair), 1)
        low = source * per_group
        match = (lane >= low) & (lane < low + per_group)
        match = match & (lax.shift_right_logical(pairs[1:2, :], 3) == wanted)
        first = jnp.max(jnp.where(match, pairs[0:1, :] & 7, -1), axis=1, keepdims=True)
        second = jnp.max(jnp.where(match, pairs[1:2, :] & 7, -1), axis=1, keepdims=True)
        column = lax.broadcasted_iota(jnp.int32, (grid.shape[0], BLK), 1)
        tab_vmem[...] = jnp.where(
            column == 0, first, jnp.where(column == 1, second, jnp.where(column == 2, ry, rz))
        )
        copy = pltpu.make_async_copy(tab_vmem, tab, tab_sem)
        copy.start()
        copy.wait()
        lane_tile = lax.broadcasted_iota(jnp.int32, (1, BLK), 1) // rows_x
        for b in range(1, nb):
            for t in range(counts[b]):
                p = base[b - 1] + t
                first = tab[p, 0]
                key = jnp.where(first >= 0, first + BPD * tab[p, 2], -1)
                line = pl.ds(group0[b] + t // per_line, 1)
                held = jnp.full((1, BLK), -1, jnp.int32) if t % per_line == 0 else keys[line, :]
                keys[line, :] = jnp.where(lane_tile == t % per_line, key, held)

    def partial_scores(b):
        if b == 0:
            for k in range(BPD):
                s = dot_tn(own[k], own[k])
                part[b][:, :, k] = s.reshape(2, xs, rows_x, BLK)
            return
        for t, (ry, rz) in enumerate(plan[b - 1]):
            p = base[b - 1] + t
            first = jnp.maximum(tab[p, 0], 0)
            second = jnp.maximum(tab[p, 1], 0)
            s = dot_tn(rowbuf[ry][first], colbuf[rz][second])
            part[b][:, :, t] = s.reshape(2, xs, rows_x, BLK)

    def stage1(b):
        inflight[b] = [
            send(part[b].at[other], from_core[b], c1_send.at[b], c1_recv.at[b], at_core)
        ]

    def x_send(b, i, src, dst, r):
        return send(src, dst, x_sems[0].at[b, i], x_sems[1].at[b, i], at_x(r))

    def stage2(b):
        inflight[b][0].wait_recv()
        part[b][core] = part[b][core] + from_core[b][...]
        inflight[b] = [
            x_send(b, r, part[b].at[core, x_of(r)], from_x[b].at[r - 1], r) for r in range(1, xs)
        ]

    def reduce_rows(b):
        for copy in inflight[b]:
            copy.wait_recv()
        total = part[b][core, x_here]
        for r in range(1, xs):
            total = total + from_x[b][r - 1]
        score[b][core, x_here] = total * scale

    def spread_rows(b):
        mine = score[b].at[core, x_here]
        inflight[b] = [x_send(b, xs + r, mine, mine, r) for r in range(1, xs)]

    def row_partials(b):
        mine = score[b][core, x_here]
        n = counts[b]
        if b == 0:
            row = lax.broadcasted_iota(jnp.int32, mine.shape, 1) + (core * xs + x_here) * rows_x
            values = jnp.where(row == lax.broadcasted_iota(jnp.int32, mine.shape, 2), NEG, mine)
        else:
            values = mine
        top = jnp.max(values, axis=1, keepdims=True)
        total = jnp.sum(jnp.exp(values - top), axis=1, keepdims=True)
        cols = (top + jnp.log(total)).reshape(n, BLK)
        if b == 0:
            diag_stat[...] = cols
            return
        col_stat[pl.ds(base[b - 1], n), :] = cols
        flat = mine.reshape(n * rows_x, BLK)
        for g in range(-(-n // per_line)):
            lines = flat[g * BLK : (g + 1) * BLK]
            if lines.shape[0] < BLK:
                lines = jnp.concatenate([lines, jnp.zeros((BLK - lines.shape[0], BLK), F32)], axis=0)
            row_stat[pl.ds(group0[b] + g, 1), :] = lse_rows(lines.T)

    def stage3(b):
        reduce_rows(b)
        spread_rows(b)
        row_partials(b)

    def stage4(b):
        for copy in inflight[b]:
            copy.wait_recv()
        inflight[b] = [
            send(score[b].at[core], score[b].at[core], c4_send.at[b], c4_recv.at[b], at_core)
        ]

    def stage5(b):
        inflight[b][0].wait_recv()

    def tile(b, t):
        return score[b][:, :, t].reshape(BLK, BLK)

    eye = lax.broadcasted_iota(jnp.int32, (BLK, BLK), 0) == lax.broadcasted_iota(
        jnp.int32, (BLK, BLK), 1
    )

    stages = [stage1, stage2, stage3, stage4, stage5]
    progress = {}

    def tick():
        for b in sorted(progress):
            if progress[b] < len(stages):
                stages[progress[b]](b)
                progress[b] += 1

    for e in range(min(2, events)):
        for f in range(4):
            gather_send(f, e)
    partial_scores(0)
    progress[0] = 0
    tick()
    slot_tables()
    tick()
    for e in range(events):
        for f in range(4):
            gathers[f][e].wait_recv()
            if e + 2 < events:
                gather_send(f, e + 2)
        b = half if e == events - 1 else ((e + 1) // 2 if e % 2 == 1 else 0)
        if b:
            partial_scores(b)
            if b >= half - 1:
                stage1(b)
                stage2(b)
            else:
                progress[b] = 0
        tick()
        tick()
    while any(p < len(stages) for p in progress.values()):
        tick()
    tail = [b for b in (half - 1, half) if b >= 1]
    block_id = lax.broadcasted_iota(jnp.int32, (BPD, BLK), 0)

    def over_lanes(values, combine):
        shift = BLK // 2
        while shift >= rows_x:
            values = combine(values, pltpu.roll(values, shift, 1))
            shift //= 2
        return values

    def col_merge(r, b_from, b_to, more):
        found = list(more)
        for o in range(side):
            if (o, r) in pos and base[b_from] <= pos[(o, r)] < base[b_to]:
                p = pos[(o, r)]
                line = jnp.broadcast_to(col_stat[pl.ds(p, 1), :], (BPD, BLK))
                found.append(jnp.where(block_id == tab[p, 1], line, NEG))
        return merge(found) if found else None

    def row_merge(r, b_from, b_to, more):
        found = []
        for b in range(b_from, b_to):
            for g in range(group0[b + 1], group0[b + 1] + -(-counts[b + 1] // per_line)):
                if all(plan[b][t][0] != r for t in range(counts[b + 1]) if t // per_line == g - group0[b + 1]):
                    continue
                line = jnp.broadcast_to(row_stat[pl.ds(g, 1), :], (BPD, BLK))
                key = jnp.broadcast_to(keys[pl.ds(g, 1), :], (BPD, BLK))
                found.append(jnp.where(key == block_id + BPD * r, line, NEG))
        if not found:
            return merge(more) if more else None
        top = over_lanes(functools.reduce(jnp.maximum, found), jnp.maximum)
        total = functools.reduce(jnp.add, [jnp.exp(v - top) for v in found])
        return merge(list(more) + [top + jnp.log(over_lanes(total, jnp.add))])

    for b in tail:
        if b == half:
            for axis, combine in ((1, col_merge), (0, row_merge)):
                for r in range(side):
                    early = combine(r, 0, half - 1, [])
                    if early is not None:
                        stat_send[axis, r] = early
        reduce_rows(b)
        if b == half:
            spread_rows(b)
        row_partials(b)

    def exchange(step, axis, source, slots):
        return [
            send(
                source(r),
                slots.at[axis, (-r) % side],
                l_send.at[step, axis, r],
                l_recv.at[step, axis, r],
                ahead[axis](r),
            )
            for r in range(1, side)
        ]

    def has_early(axis, r):
        mine = [pos[slot] for slot in pos if slot[1 if axis == 1 else 0] == r]
        return any(p < base[half - 1] for p in mine)

    exchanged = []
    for axis, combine in ((1, col_merge), (0, row_merge)):
        for r in range(side):
            early = [stat_send[axis, r]] if has_early(axis, r) else []
            stat_send[axis, r] = combine(r, half - 1, half, early)
        exchanged += exchange(0, axis, lambda r, axis=axis: stat_send.at[axis, r], stat_recv)
    for copy in exchanged:
        copy.wait_recv()
    dp_stat[0, 0] = merge([stat_send[0, 0]] + [stat_recv[0, r] for r in range(1, side)])
    dp_stat[0, 1] = merge(
        [diag_stat[...], stat_send[1, 0]] + [stat_recv[1, r] for r in range(1, side)]
    )
    exchanged = [
        send(
            dp_stat.at[0],
            dp_stat.at[2 * xs - r],
            dp_sems[0].at[r],
            dp_sems[1].at[r],
            at_dp(r),
        )
        for r in range(1, 2 * xs)
    ]
    for b in tail[:-1]:
        spread_rows(b)
    for copy in exchanged:
        copy.wait_recv()
    lane_group = lax.broadcasted_iota(jnp.int32, (BPD, BLK), 1) // rows_x
    found = []
    for r in range(2 * xs):
        source = lax.rem(d + r, 2 * xs)
        part_of = lax.rem(source, 2) * xs + lax.div(source, 2)
        found.append(jnp.where(lane_group == part_of, dp_stat[r, 0], NEG))
        found.append(dp_stat[r, 1])
    lse_own = merge(found)
    lse_out[...] = lse_own
    level[0, 0] = lse_own
    level[1, 0] = lse_own
    exchanged = exchange(1, 0, lambda r: level.at[0, 0], level)
    exchanged += exchange(1, 1, lambda r: level.at[1, 0], level)
    stage4(half)
    for copy in exchanged:
        copy.wait_recv()
    stage5(half)

    def two_sided(values, li, lj):
        li = jnp.broadcast_to(li, (BLK, BLK)).T
        return jnp.exp(values - li) + jnp.exp(values - lj)

    def weights(b, start=0, stop=None):
        def body(t, carry):
            p = base[b - 1] + t
            first, second = tab[p, 0], tab[p, 1]
            li = level[0, tab[p, 2], pl.ds(jnp.maximum(first, 0), 1), :]
            lj = level[1, tab[p, 3], pl.ds(jnp.maximum(second, 0), 1), :]
            w = jnp.where(first >= 0, two_sided(tile(b, t), li, lj), 0.0)
            w = w.astype(BF16)
            w_ref[p] = w
            wt_ref[p] = w.T
            return carry

        stop = counts[b] if stop is None else stop
        if b == half:
            for t in range(start, stop):
                body(t, 0)
        else:
            lax.fori_loop(start, stop, body, 0)

    def contribution(axis, rel, c):
        slots = [o for o in range(side) if (rel, o) != (0, 0)]
        for i, o in enumerate(slots):
            p = pos[(rel, o) if axis == 0 else (o, rel)]
            mine, theirs = tab[p, axis], tab[p, 1 - axis]
            lanes = pl.ds(i * BLK, BLK)
            stacked[:, lanes] = bufs[1 - axis][o][jnp.maximum(theirs, 0)]
            w = (wt_ref if axis == 0 else w_ref)[p]
            for k in range(HALF_BPD):
                wide[lanes, pl.ds(k * BLK, BLK)] = jnp.where(
                    mine == c * HALF_BPD + k, w, jnp.zeros_like(w)
                )
        depth = pl.ds(0, len(slots) * BLK)
        return jnp.dot(stacked[:, depth], wide[depth, :], preferred_element_type=F32)

    def by_block(out, offset, values):
        for k in range(HALF_BPD):
            out[offset + k] = values[:, k * BLK : (k + 1) * BLK]

    scatters = [[None] * events for _ in flows]

    def scatter_send(f, e, out):
        axis, sign = flows[f]
        scatters[f][e] = send(
            out, ring_in[f][e], rs_send.at[f, e], rs_recv.at[f, e], ahead[axis](sign % side)
        )

    for e in range(events):
        rho = half - (e + 1) // 2
        if e % 2 == 1:
            if rho == half - 1:
                stage4(rho)
                stage5(rho)
            weights(rho)
        for f, (axis, sign) in enumerate(flows):
            if e == 0 and sign > 0:
                weights(half, side * axis, side if axis == 0 else None)
            own_part = contribution(axis, (rho * sign) % side, chunk_of(sign, e))
            if e < 2:
                by_block(fresh.at[f, e], 0, own_part.astype(BF16))
                scatter_send(f, e, fresh.at[f, e])
            else:
                by_block(temp.at[f], 0, own_part)
        if e >= 2:
            for f in range(4):
                scatters[f][e - 2].wait_recv()
                out = ring_in[f][e - 2]
                out[...] = (temp[f] + out[...].astype(F32)).astype(BF16)
                scatter_send(f, e, out)

    for k in range(BPD):
        line = lse_own[k : k + 1]
        values = jnp.where(eye, NEG, tile(0, k))
        w = two_sided(values, line, line).T.astype(BF16)
        swap = lax.broadcasted_iota(jnp.int32, (BLK, BLK), 0) == partner[pl.ds(k, 1), :]
        swap = jnp.where(swap, 1.0, 0.0).astype(BF16)
        acc[k] = jnp.dot(own[k], w, preferred_element_type=F32) - 2.0 * jnp.dot(
            own[k], swap, preferred_element_type=F32
        )
    for axis in (0, 1):
        for c in (0, 1):
            rows = pl.ds(c * HALF_BPD, HALF_BPD)
            by_block(temp.at[0], 0, contribution(axis, 0, c))
            acc[rows] = acc[rows] + temp[0]
    last = [e for e in range(events) if half - (e + 1) // 2 == 1]
    for e in last[:-1]:
        for f, (axis, sign) in enumerate(flows):
            scatters[f][e].wait_recv()
            rows = pl.ds(chunk_of(sign, e) * HALF_BPD, HALF_BPD)
            acc[rows] = acc[rows] + ring_in[f][e][...].astype(F32)
    stores = []
    e = last[-1]
    for sign in (1, -1):
        pair = [f for f in range(4) if flows[f][1] == sign]
        for f in pair:
            scatters[f][e].wait_recv()
        for i in range(HALF_BPD):
            k = chunk_of(sign, e) * HALF_BPD + i
            total = acc[k]
            for f in pair:
                total = total + ring_in[f][e][i].astype(F32)
            done[k] = total.astype(BF16)
            stores.append(
                pltpu.make_async_copy(
                    done.at[k], grad_out.at[:, pl.ds(k * BLK, BLK)], out_sem.at[k]
                )
            )
            stores[-1].start()
    for copy in stores:
        copy.wait()
    for copy in started:
        copy.wait_send()


def fused(embeddings, pairs, partner, side, xs):
    width = embeddings.shape[0]
    half = side // 2
    plan = slot_plan(side)
    counts = [BPD] + [len(batch) for batch in plan]
    nb = len(counts)
    nslot = sum(counts[1:])
    events = 2 * half - 1
    rows_x = BLK // (2 * xs)
    dma = pltpu.SemaphoreType.DMA
    blocks = pltpu.VMEM((BPD, width, BLK), BF16)
    chunk = pltpu.VMEM((HALF_BPD, width, BLK), BF16)
    stats = pltpu.VMEM((2, side, BPD, BLK), F32)
    scratch = [blocks] * (2 * side - 1)
    scratch += [pltpu.VMEM((2, xs, n, rows_x, BLK), F32) for n in counts]
    scratch += [pltpu.VMEM((xs, n, rows_x, BLK), F32) for n in counts]
    scratch += [pltpu.VMEM((xs - 1, n, rows_x, BLK), F32) for n in counts]
    scratch += [pltpu.VMEM((2, xs, n, rows_x, BLK), F32) for n in counts]
    padded = -(-nslot // 8) * 8
    scratch += [pltpu.VMEM((padded, BLK), F32)] * 2 + [pltpu.VMEM((BPD, BLK), F32)]
    scratch += [stats] * 3 + [pltpu.VMEM((nslot, BLK, BLK), BF16)] * 2
    scratch += [pltpu.VMEM((padded, BLK), jnp.int32), pltpu.VMEM((2 * xs, 2, BPD, BLK), F32)]
    scratch += [
        pltpu.VMEM((side * BLK, HALF_BPD * BLK), BF16),
        pltpu.VMEM((width, side * BLK), BF16),
        pltpu.VMEM((4, HALF_BPD, width, BLK), F32),
        pltpu.VMEM((BPD, width, BLK), F32),
        pltpu.VMEM((4, 2, HALF_BPD, width, BLK), BF16),
        blocks,
        pltpu.VMEM((padded, BLK), jnp.int32),
        pltpu.SMEM((padded, BLK), jnp.int32),
    ]
    scratch += [chunk] * (4 * events)
    scratch += [dma((4, events))] * 2 + [dma((nb,))] * 2 + [dma((nb, 2 * xs))] * 2
    scratch += [dma((nb,))] * 2 + [dma((2, 2, side))] * 2 + [dma((4, events))] * 2
    scratch += [dma((BPD,))] * 2 + [dma(())] + [dma((2 * xs,))] * 2
    anywhere = pl.BlockSpec(memory_space=pl.ANY)
    vmem = pl.BlockSpec(memory_space=pltpu.VMEM)
    flops = 2 * BLK * BLK * width * (counts[0] * 4 + nslot * (1 + 2 * BPD))
    return pl.pallas_call(
        functools.partial(kernel, side, xs, 2.0 / math.sqrt(D)),
        out_shape=(
            jax.ShapeDtypeStruct((BPD, BLK), F32),
            jax.ShapeDtypeStruct((width, BPD * BLK), BF16),
        ),
        in_specs=[anywhere, vmem, vmem, vmem],
        out_specs=(vmem, anywhere),
        scratch_shapes=scratch,
        compiler_params=pltpu.CompilerParams(
            collective_id=0, has_side_effects=True, vmem_limit_bytes=VMEM_BYTES
        ),
        cost_estimate=pl.CostEstimate(
            flops=flops, bytes_accessed=4 * embeddings.size, transcendentals=6 * nslot * BLK * BLK
        ),
    )(embeddings, pairs, partner, jnp.asarray(slot_grid(side)))


def per_device(embeddings, pairs, partner):
    rows_here, width = embeddings.shape
    side = math.isqrt(lax.axis_size("tensor"))
    xs = lax.axis_size("dp") // 2
    lse, grad = fused(
        embeddings.T, pairs.T, (partner % BLK).reshape(BPD, BLK), side, xs
    )
    return lse.reshape(rows_here), grad.T


def solution(mesh):
    in_specs = (P("tensor", "dp"), P(), P("tensor"))
    out_specs = (P("tensor"), P("tensor", "dp"))
    return jax.shard_map(
        per_device, mesh=mesh, in_specs=in_specs, out_specs=out_specs, check_vma=False
    )
```
